32 devices in a mesh: grp: 2 (over x), dev: 16 (over z, y, core).
Axes of the slice: x: 2, y: 2, z: 4, core: 2. Of those that a mesh axis runs over, the one named last changes fastest.
Arguments:
- populations: float32 [19, 128, 64, 256], P(None, 'dev', 'grp'), may hold values from 0 to 0.5, as said below
- heat_pops: float32 [7, 128, 64, 256], P(None, 'dev', 'grp'), may hold values from 0 to 0.75, as said below
- solid_temp: float32 [128, 64, 256], P('dev', 'grp'), may hold values from 0.2 to 2
- conductivity: float32 [128, 64, 256], P('dev', 'grp'), may hold values from 1 to 10
- pore_mask: int32 [128, 64, 256], P('dev', 'grp'), may hold values 0 or 1
Outputs:
- new_pops: float32 [19, 128, 64, 256], P(None, 'dev', 'grp')
- new_heat: float32 [7, 128, 64, 256], P(None, 'dev', 'grp')
- new_solid: float32 [128, 64, 256], P('dev', 'grp')
The draws below stay inside these ranges and needn't reach their ends.
Inputs may be any that keep to these rules, and one draw needn't show every extreme that they name: `populations`: each flow population is its lattice weight times a factor of order one, so the density is positive. `heat_pops`: each thermal population is its lattice weight times a positive factor.
All inputs are finite; a program needn't handle non-finite values. No bound on the sum of `pore_mask` on one device may be relied on, other than what follows from the above.
Results may differ from the reference program's by a relative error of at most 0.00002.
Values sent between devices are 32-bit elements; how exact they have to be, the bound alone decides.
No kernel may reach another device: no remote copies, remote signals or barrier semaphores. Data moves between devices by JAX's collectives and lax.ppermute only.
A program may use at most 128 MiB of HBM per device.

```python
import math
import jax
import jax.numpy as jnp
import numpy as np

ITERS = 4
NX = 128
NZ = 64
NY = 256


def draw_populations(key, part):
    own_key = jax.random.fold_in(key, 11)
    weights = jnp.array([1.0 / 3.0] + [1.0 / 18.0] * 6 + [1.0 / 36.0] * 12, jnp.float32)
    factor = jax.random.uniform(own_key, (19, NX, NZ, NY), jnp.float32, 0.75, 1.25)
    return weights[:, None, None, None] * factor


def draw_heat_pops(key, part):
    own_key = jax.random.fold_in(key, 72)
    weights = jnp.array([0.25] + [0.125] * 6, jnp.float32)
    factor = jax.random.uniform(own_key, (7, NX, NZ, NY), jnp.float32, 0.4, 2.0)
    return weights[:, None, None, None] * factor


def place_ends(entries, rng, low, high):
    dims = entries.shape
    spot = [jax.random.randint(jax.random.fold_in(rng, axis), (), 0, dims[axis]) for axis in range(len(dims))]
    entries = entries.at[tuple(spot)].set(low)
    longest = dims.index(max(dims))
    spot[longest] = (spot[longest] + 1) % dims[longest]
    return entries.at[tuple(spot)].set(high)


def steps_of(rng, dims, cuts, least, largest):
    def one(position, parts):
        draws = jax.random.uniform(jax.random.fold_in(jax.random.fold_in(rng, 6), position), (parts,), jnp.float32, least / len(cuts), largest / len(cuts))
        return jnp.repeat(jnp.exp(draws), dims[position] // parts).reshape((-1,) + (1,) * (len(dims) - position - 1))

    level = one(*cuts[0])
    for cut in cuts[1:]:
        level = level * one(*cut)
    return level


def setup_inputs(seed: int = 0) -> dict:
    arg_keys = jax.random.split(jax.random.key(seed), 6)
    populations = draw_populations(jax.random.fold_in(arg_keys[5], 71), 0)
    heat_pops = draw_heat_pops(jax.random.fold_in(arg_keys[5], 71), 0)
    solid_temp = jnp.clip(0.2 + 1.8 * jax.random.uniform(arg_keys[2], (NX, NZ, NY), jnp.float32) ** steps_of(arg_keys[2], (NX, NZ, NY), ((0, 16), (1, 2)), -0.2, 0.2), 0.2, 2.0)
    conductivity = jnp.clip(jnp.exp(math.log(10.0) - 2.3025851 * jax.random.uniform(arg_keys[3], (NX, NZ, NY), jnp.float32) ** steps_of(arg_keys[3], (NX, NZ, NY), ((0, 16), (1, 2)), -0.2, 0.2)), 1.0, 10.0)
    pore_mask = place_ends((jax.random.randint(arg_keys[4], (NX, NZ, NY), 0, 4) < 1).astype(jnp.int32), jax.random.fold_in(arg_keys[4], 1), 0, 1)
    return {"populations": populations, "heat_pops": heat_pops, "solid_temp": solid_temp, "conductivity": conductivity, "pore_mask": pore_mask}


flow_dirs = np.array([[0, 0, 0], [1, 0, 0], [-1, 0, 0], [0, 1, 0], [0, -1, 0], [0, 0, 1], [0, 0, -1],
                      [1, 1, 0], [-1, -1, 0], [1, -1, 0], [-1, 1, 0], [1, 0, 1], [-1, 0, -1], [1, 0, -1],
                      [-1, 0, 1], [0, 1, 1], [0, -1, -1], [0, 1, -1], [0, -1, 1]])
flow_weights = [1.0 / 3.0] + [1.0 / 18.0] * 6 + [1.0 / 36.0] * 12
flow_opposite = [0, 2, 1, 4, 3, 6, 5, 8, 7, 10, 9, 12, 11, 14, 13, 16, 15, 18, 17]
heat_weights = [0.25] + [0.125] * 6
relax_flow = 0.8
relax_heat = 0.7
jump_ratio = 0.3
film_coeff = 0.5
cheb_theta = 61.0
cheb_delta = 60.0


def upwind(field, index):
    dirc = flow_dirs[index]
    return jnp.roll(field, (int(dirc[0]), int(dirc[2]), int(dirc[1])), axis=(0, 1, 2))


def reference(populations, heat_pops, solid_temp, conductivity, pore_mask):
    pore = pore_mask.astype(jnp.float32)
    solid = 1.0 - pore
    density = jnp.sum(populations, axis=0)
    vel = [jnp.sum(populations * jnp.asarray(flow_dirs[:, a], jnp.float32)[:, None, None, None], axis=0) / density for a in range(3)]
    fluid_temp = jnp.sum(heat_pops, axis=0)
    usq = vel[0] * vel[0] + vel[1] * vel[1] + vel[2] * vel[2]
    flow_star = []
    heat_star = []
    for index in range(19):
        dirc = flow_dirs[index]
        cdot = float(dirc[0]) * vel[0] + float(dirc[1]) * vel[1] + float(dirc[2]) * vel[2]
        equil = flow_weights[index] * density * (1.0 + 3.0 * cdot + 4.5 * cdot * cdot - 1.5 * usq)
        flow_star.append(populations[index] - (populations[index] - equil) / relax_flow)
        if index < 7:
            hequil = heat_weights[index] * fluid_temp * (1.0 + 4.0 * cdot)
            heat_star.append(heat_pops[index] - (heat_pops[index] - hequil) / relax_heat)
    new_flow = []
    new_hot = []
    for index in range(19):
        near_pore = upwind(pore, index)
        moved = near_pore * upwind(flow_star[index], index) + (1.0 - near_pore) * flow_star[flow_opposite[index]]
        new_flow.append(pore * moved + solid * populations[index])
        if index < 7:
            near_solid = upwind(solid_temp, index)
            wall_temp = near_solid + jump_ratio * (fluid_temp - near_solid)
            hmoved = near_pore * upwind(heat_star[index], index) + (1.0 - near_pore) * (
                -heat_star[flow_opposite[index]] + 2.0 * heat_weights[index] * wall_temp)
            new_hot.append(pore * hmoved + solid * heat_pops[index])
    new_pops = jnp.stack(new_flow, axis=0)
    new_heat = jnp.stack(new_hot, axis=0)
    temp_new = pore * jnp.sum(new_heat, axis=0)
    inflow = jnp.zeros_like(solid_temp)
    for index in range(1, 7):
        inflow = inflow + upwind(pore, index) * film_coeff * (upwind(temp_new, index) - solid_temp)
    source = solid_temp + solid * inflow
    faces = []
    for index in range(1, 7):
        knear = upwind(conductivity, index)
        faces.append(solid * upwind(solid, index) * 2.0 * conductivity * knear / (conductivity + knear))

    def operate(field):
        total = field
        for index in range(1, 7):
            total = total + faces[index - 1] * (field - upwind(field, index))
        return total

    sigma = cheb_theta / cheb_delta
    iterate = solid_temp
    resid = source - operate(iterate)
    ratio = 1.0 / sigma
    step = resid / cheb_theta
    for sweep in range(ITERS):
        iterate = iterate + step
        if sweep + 1 < ITERS:
            resid = resid - operate(step)
            ratio_next = 1.0 / (2.0 * sigma - ratio)
            step = ratio_next * ratio * step + (2.0 * ratio_next / cheb_delta) * resid
            ratio = ratio_next
    new_solid = solid * iterate + pore * solid_temp
    return new_pops, new_heat, new_solid
```

```python
import functools

import jax
import jax.numpy as jnp
from jax import lax
from jax.experimental import pallas as pl
from jax.experimental.pallas import tpu as pltpu
from jax.sharding import PartitionSpec as P

ITERS = 4
DIRS = (
    (0, 0, 0),
    (1, 0, 0),
    (-1, 0, 0),
    (0, 1, 0),
    (0, -1, 0),
    (0, 0, 1),
    (0, 0, -1),
    (1, 1, 0),
    (-1, -1, 0),
    (1, -1, 0),
    (-1, 1, 0),
    (1, 0, 1),
    (-1, 0, -1),
    (1, 0, -1),
    (-1, 0, 1),
    (0, 1, 1),
    (0, -1, -1),
    (0, 1, -1),
    (0, -1, 1),
)
OPP = (0, 2, 1, 4, 3, 6, 5, 8, 7, 10, 9, 12, 11, 14, 13, 16, 15, 18, 17)
PAIRS = ((1, 2), (3, 4), (5, 6), (7, 8), (9, 10), (11, 12), (13, 14), (15, 16), (17, 18))
ZPAIRS = ((5, 6), (11, 12), (14, 13), (15, 16), (18, 17))
ZSLOT = {5: (1, 2), 6: (1, 2), 11: (1, 3), 12: (1, 3), 14: (2, 0), 13: (2, 0), 15: (2, 1), 16: (2, 1), 18: (2, 2), 17: (2, 2)}
XHIGH = (1, 7, 9, 11, 13)
XLOW = (2, 8, 10, 12, 14)
W0, W1, W2 = 1.0 / 3.0, 1.0 / 18.0, 1.0 / 36.0
RELAX_FLOW = 0.8
RELAX_HEAT = 0.7
JUMP = 0.3
FILM = 0.5
THETA = 61.0
DELTA = 60.0
WALL_OWN = 0.25 * JUMP
WALL_NEAR = 0.25 * (1.0 - JUMP)
DEEP = 4
TILE = 8

VM = pl.BlockSpec(memory_space=pltpu.VMEM)
ANY = pl.BlockSpec(memory_space=pl.ANY)


def call(body, outs, args, in_specs=None, out_specs=None, scratch=(), aliases=None, limit=4 << 20):
    return pl.pallas_call(
        body,
        out_shape=[jax.ShapeDtypeStruct(shape, jnp.float32) for shape in outs],
        in_specs=in_specs or [VM] * len(args),
        out_specs=out_specs or [VM] * len(outs),
        scratch_shapes=list(scratch),
        input_output_aliases=aliases or {},
        compiler_params=pltpu.CompilerParams(vmem_limit_bytes=limit),
    )(*args)


def rows8(shape):
    return lax.broadcasted_iota(jnp.int32, shape, 0)


def collide_body(pops, heat, ts, cond, pore, flow, hot, tsm, km):
    nx, nz = ts.shape[0], ts.shape[1] // TILE

    def step(i, carry):
        x = i // nz
        rows = pl.ds(pl.multiple_of((i % nz) * TILE, TILE), TILE)
        is_pore = pore[x, rows, :] != 0
        tsm[x, rows, :] = jnp.where(is_pore, 0.0, ts[x, rows, :])
        km[x, rows, :] = jnp.where(is_pore, 0.0, cond[x, rows, :])
        p = [pops[d, x, rows, :] for d in range(19)]
        diff = [p[a] - p[b] for a, b in PAIRS]
        rho = p[0]
        for a, b in PAIRS:
            rho = rho + (p[a] + p[b])
        inv = 1.0 / rho
        ux = (diff[0] + diff[3] + diff[4] + diff[5] + diff[6]) * inv
        uy = (diff[1] + diff[3] - diff[4] + diff[7] + diff[8]) * inv
        uz = (diff[2] + diff[5] - diff[6] + diff[7] - diff[8]) * inv
        base = 1.0 - 1.5 * (ux * ux + uy * uy + uz * uz)
        keep = 1.0 - 1.0 / RELAX_FLOW
        flow[0, x, rows, :] = jnp.where(is_pore, (W0 / RELAX_FLOW) * rho * base + keep * p[0], p[0])
        speeds = (ux, uy, uz, ux + uy, ux - uy, ux + uz, ux - uz, uy + uz, uy - uz)
        scaled1 = (W1 / RELAX_FLOW) * rho
        scaled2 = (W2 / RELAX_FLOW) * rho
        for n, (a, b) in enumerate(PAIRS):
            scaled = scaled1 if n < 3 else scaled2
            cu = speeds[n]
            even = scaled * (base + 4.5 * (cu * cu))
            odd = scaled * (3.0 * cu)
            flow[a, x, rows, :] = jnp.where(is_pore, (even + odd) + keep * p[a], p[a])
            flow[b, x, rows, :] = jnp.where(is_pore, (even - odd) + keep * p[b], p[b])
        h = [heat[d, x, rows, :] for d in range(7)]
        temp = h[0] + (h[1] + h[2]) + (h[3] + h[4]) + (h[5] + h[6])
        hkeep = 1.0 - 1.0 / RELAX_HEAT
        hot[0, x, rows, :] = jnp.where(is_pore, (0.25 / RELAX_HEAT) * temp + hkeep * h[0], h[0])
        even = (0.125 / RELAX_HEAT) * temp
        for n in range(3):
            a, b = PAIRS[n]
            odd = even * (4.0 * speeds[n])
            hot[a, x, rows, :] = jnp.where(is_pore, (even + odd) + hkeep * h[a], h[a])
            hot[b, x, rows, :] = jnp.where(is_pore, (even - odd) + hkeep * h[b], h[b])
        return carry

    lax.fori_loop(0, nx * nz, step, 0)


def edge_tile(low, high, row):
    return jnp.where(row < DEEP, low, high)


def pack_pairs(pairs, row):
    out = None
    for j, (low, high) in enumerate(pairs):
        if j:
            low, high = pltpu.roll(low, j, 0), pltpu.roll(high, TILE - j, 0)
        both = jnp.where(row < DEEP, low, high)
        out = both if out is None else jnp.where((row == j) | (row == TILE - 1 - j), both, out)
    return out


def heat_body(hot, flow, tsm, km, new_heat, temp, bounce, zmsg):
    nx, nz, ny = tsm.shape
    rowz = rows8((nz, ny))
    row = rows8((TILE, ny))
    first, last = slice(0, TILE), slice(nz - TILE, nz)
    for x in range(nx):
        t = tsm[x]
        is_pore = t == 0.0
        g = [hot[d, x] for d in range(7)]
        own = WALL_OWN * (g[0] + (g[1] + g[2]) + (g[3] + g[4]) + (g[5] + g[6]))
        new_heat[0, x] = g[0]
        total = g[0]

        def arrive(d, near, moved):
            return jnp.where(near == 0.0, moved, (own - g[OPP[d]]) + WALL_NEAR * near)

        for d in (1, 2):
            src = x - DIRS[d][0]
            if 0 <= src < nx:
                got = arrive(d, tsm[src], hot[d, src])
                total = total + got
                new_heat[d, x] = jnp.where(is_pore, got, g[d])
            else:
                new_heat[d, x] = g[d]
                bounce[0 if x == 0 else 1] = own - g[OPP[d]]
        for d in (3, 4):
            by = DIRS[d][1] % ny
            got = arrive(d, pltpu.roll(t, by, 1), pltpu.roll(g[d], by, 1))
            total = total + got
            new_heat[d, x] = jnp.where(is_pore, got, g[d])
        for d in (5, 6):
            by = DIRS[d][2] % nz
            got = arrive(d, pltpu.roll(t, by, 0), pltpu.roll(g[d], by, 0))
            inside = rowz != (0 if d == 5 else nz - 1)
            total = total + jnp.where(inside, got, 0.0)
            new_heat[d, x] = jnp.where(is_pore & inside, got, g[d])
        total = jnp.where(is_pore, total, 0.0)
        temp[x] = total
        zmsg[x] = edge_tile(total[first], total[last], row)
        pairs = [(g[6][first], g[5][last]), ((own - g[6])[first], (own - g[5])[last])]
        for up, down in ZPAIRS:
            pairs.append((flow[down, x, first, :], flow[up, x, last, :]))
        zmsg[nx + x] = pack_pairs(pairs[:4], row)
        zmsg[2 * nx + x] = pack_pairs(pairs[4:], row)
        zmsg[3 * nx + x] = edge_tile(t[first], t[last], row)
        zmsg[4 * nx + x] = edge_tile(km[x, first, :], km[x, last, :], row)
    ends = (hot[2, 0], hot[1, nx - 1], bounce[0], bounce[1])
    for n, v in enumerate(ends):
        zmsg[5 * nx + n] = edge_tile(v[first], v[last], row)


def zjoin_body(mine, theirs, temp, hot, tsm, km, bounce, flow, heat_in, heat_ends, low, high, flow_low, flow_high):
    nx, nz, ny = tsm.shape
    row = rows8((TILE, ny))
    edge = (row == 0) | (row == TILE - 1)
    first, last, halo = slice(0, TILE), slice(nz - TILE, nz), slice(nz, nz + TILE)
    half = nx // 2

    def swap(v):
        return jnp.where(row < DEEP, pltpu.roll(v, 1, 0), pltpu.roll(v, TILE - 1, 0))

    def slot1(v):
        return jnp.where(row < DEEP, pltpu.roll(v, TILE - 1, 0), pltpu.roll(v, 1, 0))

    for x in range(nx):
        my_t, their_t = mine[3 * nx + x], theirs[3 * nx + x]
        my_p, their_p = mine[nx + x], theirs[nx + x]
        near = swap(their_t)
        got = jnp.where(near == 0.0, swap(their_p), slot1(my_p) + WALL_NEAR * near)
        mine_in = edge & (my_t == 0.0)
        add = jnp.where(mine_in, got, 0.0)
        near = swap(my_t)
        back = jnp.where(near == 0.0, swap(my_p), slot1(their_p) + WALL_NEAR * near)
        back = jnp.where(edge & (their_t == 0.0), back, 0.0)
        heat_ends[0, x] = jnp.where(mine_in & (row == 0), got, heat_in[5, x, first, :])
        heat_ends[1, x] = jnp.where(mine_in & (row == TILE - 1), got, heat_in[6, x, last, :])
        out, n = (low, x) if x < half else (high, x - half)
        out[n, 0:nz, :] = temp[x]
        out[n, first, :] = temp[x, first, :] + jnp.where(row == 0, add, 0.0)
        out[n, last, :] = temp[x, last, :] + jnp.where(row == TILE - 1, add, 0.0)
        out[n, halo, :] = theirs[x] + back
        out[DEEP + 2 + n, 0:nz, :] = tsm[x]
        out[DEEP + 2 + n, halo, :] = their_t
        out[2 * DEEP + 2 + n, 0:nz, :] = km[x]
        out[2 * DEEP + 2 + n, halo, :] = theirs[4 * nx + x]
    for side, out in ((0, low), (1, high)):
        x = side * (nx - 1)
        out[DEEP, 0:nz, :] = hot[2 - side, x]
        out[DEEP, halo, :] = theirs[5 * nx + side]
        out[DEEP + 1, 0:nz, :] = bounce[side]
        out[DEEP + 1, halo, :] = theirs[5 * nx + 2 + side]
    for x, dirs, out in ((0, XLOW, flow_low), (nx - 1, XHIGH, flow_high)):
        for n, d in enumerate(dirs):
            out[n, 0:nz, :] = flow[d, x]
            if d in ZSLOT:
                block, j = ZSLOT[d]
                v = theirs[block * nx + x]
                by = j if DIRS[d][2] > 0 else TILE - j
                out[n, halo, :] = pltpu.roll(v, by % TILE, 0) if by % TILE else v
            else:
                out[n, halo, :] = jnp.zeros((TILE, ny), jnp.float32)


def conduct_body(low, high, from_low, from_high, hot, ts, heat_in, new_heat, new_solid, temp, fx, fy, fz, resid, step_a, step_b, ends, sems):
    nx, nz, ny = ts.shape
    ext = low.shape[1]
    planes = nx + 2 * DEEP

    def at(field, p):
        part, n = ((from_low, p), (low, p - DEEP), (high, p - 2 * DEEP), (from_high, p - 3 * DEEP))[p // DEEP]
        return part[{"temp": 0, "ts": DEEP + 2, "km": 2 * DEEP + 2}[field] + n]

    def join(below, above, p_low, p_high):
        t_low, t_high = at("ts", p_low), at("ts", p_high)
        up = jnp.where(t_low == 0.0, below[DEEP], above[DEEP + 1] + WALL_NEAR * t_low)
        down = jnp.where(t_high == 0.0, above[DEEP], below[DEEP + 1] + WALL_NEAR * t_high)
        temp[p_high] = jnp.where(t_high == 0.0, at("temp", p_high) + up, 0.0)
        temp[p_low] = jnp.where(t_low == 0.0, at("temp", p_low) + down, 0.0)
        return up, down

    for p in range(planes):
        if p not in (DEEP - 1, DEEP, DEEP + nx - 1, DEEP + nx):
            temp[p] = at("temp", p)
    up, _ = join(from_low, low, DEEP - 1, DEEP)
    _, down = join(high, from_high, DEEP + nx - 1, DEEP + nx)
    own = slice(0, nz)
    ends[0] = jnp.where(at("ts", DEEP)[own] == 0.0, up[own], hot[1, 0])
    ends[1] = jnp.where(at("ts", DEEP + nx - 1)[own] == 0.0, down[own], hot[2, nx - 1])
    copies = [
        pltpu.make_async_copy(ends.at[0], new_heat.at[1, 0], sems.at[0]),
        pltpu.make_async_copy(ends.at[1], new_heat.at[2, nx - 1], sems.at[1]),
    ]
    for copy in copies:
        copy.start()

    def face(a, b):
        return (2.0 * a) * b / jnp.maximum(a + b, 1.0)

    def net_of(p, v, below, prev, ahead):
        flux_y = fy[p] * (pltpu.roll(v, 1, 1) - v)
        flux_z = fz[p] * (pltpu.roll(v, 1, 0) - v)
        if below is None:
            below = fx[p] * (prev - v)
        above = fx[p + 1] * (v - ahead)
        net = below - above
        net = net + (flux_y - pltpu.roll(flux_y, ny - 1, 1))
        net = net + (flux_z - pltpu.roll(flux_z, ext - 1, 0))
        return net, above

    for p in range(1, planes):
        k, kp = at("km", p), at("km", p - 1)
        fx[p] = face(k, kp)
    below = None
    for p in range(1, planes - 1):
        k, t = at("km", p), at("ts", p)
        ky = pltpu.roll(k, 1, 1)
        kz = pltpu.roll(k, 1, 0)
        fy[p] = face(k, ky)
        fz[p] = face(k, kz)
        pore = jnp.where(k == 0.0, 1.0, 0.0)
        count = jnp.where(ky == 0.0, 1.0, 0.0) + jnp.where(kz == 0.0, 1.0, 0.0)
        count = count + pltpu.roll(pore, ny - 1, 1) + pltpu.roll(pore, ext - 1, 0)
        count = count + jnp.where(at("km", p - 1) == 0.0, 1.0, 0.0) + jnp.where(at("km", p + 1) == 0.0, 1.0, 0.0)
        mid = temp[p]
        near = (temp[p - 1] + temp[p + 1]) + (pltpu.roll(mid, 1, 1) + pltpu.roll(mid, ny - 1, 1))
        near = near + (pltpu.roll(mid, 1, 0) + pltpu.roll(mid, ext - 1, 0))
        net, below = net_of(p, t, below, at("ts", p - 1), at("ts", p + 1))
        r = jnp.where(k == 0.0, 0.0, FILM * (near - count * t)) + net
        resid[p] = r
        s = r / THETA
        step_a[p] = s
        if DEEP <= p < DEEP + nx:
            new_solid[p - DEEP] = ts[p - DEEP] + s[own]
    sigma = THETA / DELTA
    ratio = 1.0 / sigma
    now, later = step_a, step_b
    for sweep in range(1, ITERS):
        after = 1.0 / (2.0 * sigma - ratio)
        below = None
        for p in range(1 + sweep, planes - 1 - sweep):
            v = now[p]
            net, below = net_of(p, v, below, now[p - 1], now[p + 1])
            r = resid[p] - (v - net)
            s = (after * ratio) * v + (2.0 * after / DELTA) * r
            if sweep + 1 < ITERS:
                resid[p] = r
                later[p] = s
            if DEEP <= p < DEEP + nx:
                new_solid[p - DEEP] = new_solid[p - DEEP] + s[own]
        ratio = after
        now, later = later, now
    for copy in copies:
        copy.wait()


def flow_body(xs, ends, *refs):
    if ends:
        flow, theirs, low, high, from_low, from_high, flow_low, flow_high, held, out, buf, sems = refs
    else:
        flow, theirs, low, high, heat, heat_ends, out, heat_out, buf, sems, heat_sems = refs
    nx, nz, ny = flow.shape[1:]
    ext = low.shape[1]
    rowz = rows8((nz, ny))
    half = nx // 2
    own = slice(0, nz)
    if not ends:
        whole = pltpu.make_async_copy(heat, heat_out, heat_sems.at[0])
        whole.start()

    def tse(q):
        if q < 0:
            return from_low[2 * DEEP + 1]
        if q >= nx:
            return from_high[DEEP + 2]
        return low[DEEP + 2 + q] if q < half else high[DEEP + 2 + q - half]

    def source(d, q):
        if q < 0:
            return flow_low[XHIGH.index(d), own, :]
        if q >= nx:
            return flow_high[XLOW.index(d), own, :]
        return flow[d, q]

    def halo_row(d, q):
        up = DIRS[d][2] > 0
        if q < 0:
            n = ext - 1 if up else nz
            return flow_low[XHIGH.index(d), n : n + 1, :]
        if q >= nx:
            n = ext - 1 if up else nz
            return flow_high[XLOW.index(d), n : n + 1, :]
        block, j = ZSLOT[d]
        n = TILE - 1 - j if up else j
        return theirs[block * nx + q, n : n + 1, :]

    copies = []
    for n, x in enumerate(xs):
        slot = n % 2
        if n >= 2:
            copies[n - 2].wait()
        is_pore = tse(x)[own] == 0.0
        mids = {}
        for d in range(1, 19):
            cx, cy, cz = DIRS[d]
            q = x - cx
            t = tse(q)
            if cy:
                if (cx, cy) not in mids:
                    mids[cx, cy] = pltpu.roll(t, cy % ny, 1)
                t = mids[cx, cy]
            if cz:
                t = pltpu.roll(t, cz % ext, 0)
            both = is_pore & (t[own] == 0.0)
            v = source(d, q)
            if cz:
                v = jnp.where(rowz == (0 if cz > 0 else nz - 1), halo_row(d, q), pltpu.roll(v, cz % nz, 0))
            if cy:
                v = pltpu.roll(v, cy % ny, 1)
            still = jnp.where(is_pore, flow[OPP[d], x], flow[d, x])
            buf[slot, d] = jnp.where(both, v, still)
        buf[slot, 0] = flow[0, x]
        copy = pltpu.make_async_copy(buf.at[slot], out.at[:, x], sems.at[slot])
        copy.start()
        copies.append(copy)
    if not ends:
        whole.wait()
        for n, rows in ((0, slice(0, TILE)), (1, slice(nz - TILE, nz))):
            copies.append(pltpu.make_async_copy(heat_ends.at[n], heat_out.at[5 + n, :, rows, :], heat_sems.at[n]))
            copies[-1].start()
    for copy in copies[-2 if ends else -4 :]:
        copy.wait()


def ring(axis, by):
    count = lax.axis_size(axis)
    return [(i, (i + by) % count) for i in range(count)]


def per_device(populations, heat_pops, solid_temp, conductivity, pore_mask):
    nx, nz, ny = solid_temp.shape
    ext = nz + TILE
    field = (nx, nz, ny)
    flow, hot, tsm, km = call(
        collide_body,
        [(19, *field), (7, *field), field, field],
        [populations, heat_pops, solid_temp, conductivity, pore_mask],
    )
    new_heat, temp, bounce, zmsg = call(
        heat_body,
        [(7, *field), field, (2, nz, ny), (5 * nx + 4, TILE, ny)],
        [hot, flow, tsm, km],
    )
    if lax.axis_size("grp") == 2:
        theirs = lax.ppermute(zmsg, "grp", ring("grp", 1))
    else:
        from_below = lax.ppermute(zmsg, "grp", ring("grp", 1))
        from_above = lax.ppermute(zmsg, "grp", ring("grp", -1))
        upper = lax.broadcasted_iota(jnp.int32, zmsg.shape, 1) < DEEP
        theirs = jnp.where(upper, from_above, from_below)
    heat_ends, low, high, flow_low, flow_high = call(
        zjoin_body,
        [(2, nx, TILE, ny), (14, ext, ny), (14, ext, ny), (5, ext, ny), (5, ext, ny)],
        [zmsg, theirs, temp, hot, tsm, km, bounce, flow, new_heat],
    )
    from_low = lax.ppermute(high, "dev", ring("dev", 1))
    from_high = lax.ppermute(low, "dev", ring("dev", -1))
    flow_from_low = lax.ppermute(flow_high, "dev", ring("dev", 1))
    flow_from_high = lax.ppermute(flow_low, "dev", ring("dev", -1))
    flow_scratch = [pltpu.VMEM((2, 19, nz, ny), jnp.float32), pltpu.SemaphoreType.DMA((2,))]
    new_pops, new_heat = call(
        functools.partial(flow_body, tuple(range(1, nx - 1)), False),
        [(19, *field), (7, *field)],
        [flow, theirs, low, high, new_heat, heat_ends],
        out_specs=[ANY, ANY],
        scratch=flow_scratch + [pltpu.SemaphoreType.DMA((2,))],
        limit=6 << 20,
    )
    planes = nx + 2 * DEEP
    new_heat, new_solid = call(
        conduct_body,
        [(7, *field), field],
        [low, high, from_low, from_high, hot, solid_temp, new_heat],
        in_specs=[VM] * 6 + [ANY],
        out_specs=[ANY, VM],
        scratch=[pltpu.VMEM((planes, ext, ny), jnp.float32)] * 7
        + [pltpu.VMEM((2, nz, ny), jnp.float32), pltpu.SemaphoreType.DMA((2,))],
        aliases={6: 0},
        limit=10 << 20,
    )
    (new_pops,) = call(
        functools.partial(flow_body, (0, nx - 1), True),
        [(19, *field)],
        [flow, theirs, low, high, from_low, from_high, flow_from_low, flow_from_high, new_pops],
        in_specs=[VM] * 8 + [ANY],
        out_specs=[ANY],
        scratch=flow_scratch,
        aliases={8: 0},
        limit=6 << 20,
    )
    return new_pops, new_heat, new_solid


def solution(mesh):
    wide = P(None, "dev", "grp", None)
    flat = P("dev", "grp", None)
    return jax.shard_map(
        per_device,
        mesh=mesh,
        in_specs=(wide, wide, flat, flat, flat),
        out_specs=(wide, wide, flat),
        check_vma=False,
    )
```

```python
import functools

import jax
import jax.numpy as jnp
from jax import lax
from jax.experimental import pallas as pl
from jax.experimental.pallas import tpu as pltpu
from jax.sharding import PartitionSpec as P

ITERS = 4
DIRS = (
    (0, 0, 0),
    (1, 0, 0),
    (-1, 0, 0),
    (0, 1, 0),
    (0, -1, 0),
    (0, 0, 1),
    (0, 0, -1),
    (1, 1, 0),
    (-1, -1, 0),
    (1, -1, 0),
    (-1, 1, 0),
    (1, 0, 1),
    (-1, 0, -1),
    (1, 0, -1),
    (-1, 0, 1),
    (0, 1, 1),
    (0, -1, -1),
    (0, 1, -1),
    (0, -1, 1),
)
OPP = (0, 2, 1, 4, 3, 6, 5, 8, 7, 10, 9, 12, 11, 14, 13, 16, 15, 18, 17)
PAIRS = ((1, 2), (3, 4), (5, 6), (7, 8), (9, 10), (11, 12), (13, 14), (15, 16), (17, 18))
ZPAIRS = ((5, 6), (11, 12), (14, 13), (15, 16), (18, 17))
ZSLOT = {5: (1, 2), 6: (1, 2), 11: (1, 3), 12: (1, 3), 14: (2, 0), 13: (2, 0), 15: (2, 1), 16: (2, 1), 18: (2, 2), 17: (2, 2)}
XHIGH = (1, 7, 9, 11, 13)
XLOW = (2, 8, 10, 12, 14)
W0, W1, W2 = 1.0 / 3.0, 1.0 / 18.0, 1.0 / 36.0
RELAX_FLOW = 0.8
RELAX_HEAT = 0.7
JUMP = 0.3
FILM = 0.5
THETA = 61.0
DELTA = 60.0
WALL_OWN = 0.25 * JUMP
WALL_NEAR = 0.25 * (1.0 - JUMP)
DEEP = 4
TILE = 8

VM = pl.BlockSpec(memory_space=pltpu.VMEM)
ANY = pl.BlockSpec(memory_space=pl.ANY)
HBM = pl.BlockSpec(memory_space=pltpu.HBM)


def call(body, outs, args, in_specs=None, out_specs=None, scratch=(), aliases=None, limit=4 << 20, us=0.5):
    return pl.pallas_call(
        body,
        out_shape=[jax.ShapeDtypeStruct(shape, jnp.float32) for shape in outs],
        in_specs=in_specs or [VM] * len(args),
        out_specs=out_specs or [VM] * len(outs),
        scratch_shapes=list(scratch),
        input_output_aliases=aliases or {},
        compiler_params=pltpu.CompilerParams(vmem_limit_bytes=limit),
        cost_estimate=pl.CostEstimate(flops=0, bytes_accessed=int(us * 3e6), transcendentals=0),
    )(*args)


def rows8(shape):
    return lax.broadcasted_iota(jnp.int32, shape, 0)


def collide_body(*refs):
    sources, (flow, hot, tsm, km, rows_out), held, sems = refs[:5], refs[5:10], refs[10:15], refs[15]
    pops, heat, ts, cond, pore = held
    nx, nz, ny = tsm.shape
    row = rows8((TILE, ny))

    def fetch(n, x):
        if n < 2:
            return pltpu.make_async_copy(sources[n].at[:, x], held[n].at[:, x], sems.at[3 + n * nx + x])
        return pltpu.make_async_copy(sources[n], held[n], sems.at[n - 2])

    for n in (2, 3, 4):
        fetch(n, 0).start()
    for x in range(nx):
        for n in (0, 1):
            fetch(n, x).start()
    for n in (2, 3, 4):
        fetch(n, 0).wait()

    def plane(x, carry):
        is_pore = pore[x] != 0
        for n, (src, dst) in enumerate(((ts, tsm), (cond, km))):
            v = jnp.where(is_pore, 0.0, src[x])
            dst[x] = v
            rows_out[n * nx + x] = edge_tile(v[0:TILE], v[nz - TILE : nz], row)
        for n in (0, 1):
            fetch(n, x).wait()
        return lax.fori_loop(0, nz // TILE, lambda i, c: step(x, i, c), carry)

    def step(x, i, carry):
        rows = pl.ds(pl.multiple_of(i * TILE, TILE), TILE)
        is_pore = tsm[x, rows, :] == 0.0
        p = [pops[d, x, rows, :] for d in range(19)]
        diff = [p[a] - p[b] for a, b in PAIRS]
        rho = p[0]
        for a, b in PAIRS:
            rho = rho + (p[a] + p[b])
        inv = 1.0 / rho
        ux = (diff[0] + diff[3] + diff[4] + diff[5] + diff[6]) * inv
        uy = (diff[1] + diff[3] - diff[4] + diff[7] + diff[8]) * inv
        uz = (diff[2] + diff[5] - diff[6] + diff[7] - diff[8]) * inv
        base = 1.0 - 1.5 * (ux * ux + uy * uy + uz * uz)
        keep = 1.0 - 1.0 / RELAX_FLOW
        flow[0, x, rows, :] = jnp.where(is_pore, (W0 / RELAX_FLOW) * rho * base + keep * p[0], p[0])
        speeds = (ux, uy, uz, ux + uy, ux - uy, ux + uz, ux - uz, uy + uz, uy - uz)
        scaled1 = (W1 / RELAX_FLOW) * rho
        scaled2 = (W2 / RELAX_FLOW) * rho
        for n, (a, b) in enumerate(PAIRS):
            scaled = scaled1 if n < 3 else scaled2
            cu = speeds[n]
            even = scaled * (base + 4.5 * (cu * cu))
            odd = scaled * (3.0 * cu)
            flow[a, x, rows, :] = jnp.where(is_pore, (even + odd) + keep * p[a], p[a])
            flow[b, x, rows, :] = jnp.where(is_pore, (even - odd) + keep * p[b], p[b])
        h = [heat[d, x, rows, :] for d in range(7)]
        temp = h[0] + (h[1] + h[2]) + (h[3] + h[4]) + (h[5] + h[6])
        hkeep = 1.0 - 1.0 / RELAX_HEAT
        hot[0, x, rows, :] = jnp.where(is_pore, (0.25 / RELAX_HEAT) * temp + hkeep * h[0], h[0])
        even = (0.125 / RELAX_HEAT) * temp
        for n in range(3):
            a, b = PAIRS[n]
            odd = even * (4.0 * speeds[n])
            hot[a, x, rows, :] = jnp.where(is_pore, (even + odd) + hkeep * h[a], h[a])
            hot[b, x, rows, :] = jnp.where(is_pore, (even - odd) + hkeep * h[b], h[b])
        return carry

    lax.fori_loop(0, nx, plane, 0)


def edge_tile(low, high, row):
    return jnp.where(row < DEEP, low, high)


def pack_pairs(pairs, row):
    out = None
    for j, (low, high) in enumerate(pairs):
        if j:
            low, high = pltpu.roll(low, j, 0), pltpu.roll(high, TILE - j, 0)
        both = jnp.where(row < DEEP, low, high)
        out = both if out is None else jnp.where((row == j) | (row == TILE - 1 - j), both, out)
    return out


def heat_body(hot, flow, tsm, rows_in, new_heat, temp, bounce, zmsg):
    nx, nz, ny = tsm.shape
    rowz = rows8((nz, ny))
    row = rows8((TILE, ny))
    first, last = slice(0, TILE), slice(nz - TILE, nz)
    for x in range(nx):
        t = tsm[x]
        is_pore = t == 0.0
        g = [hot[d, x] for d in range(7)]
        own = WALL_OWN * (g[0] + (g[1] + g[2]) + (g[3] + g[4]) + (g[5] + g[6]))
        new_heat[0, x] = g[0]
        total = g[0]

        def arrive(d, near, moved):
            return jnp.where(near == 0.0, moved, (own - g[OPP[d]]) + WALL_NEAR * near)

        for d in (1, 2):
            src = x - DIRS[d][0]
            if 0 <= src < nx:
                got = arrive(d, tsm[src], hot[d, src])
                total = total + got
                new_heat[d, x] = jnp.where(is_pore, got, g[d])
            else:
                new_heat[d, x] = g[d]
                bounce[0 if x == 0 else 1] = own - g[OPP[d]]
        for d in (3, 4):
            by = DIRS[d][1] % ny
            got = arrive(d, pltpu.roll(t, by, 1), pltpu.roll(g[d], by, 1))
            total = total + got
            new_heat[d, x] = jnp.where(is_pore, got, g[d])
        for d in (5, 6):
            by = DIRS[d][2] % nz
            got = arrive(d, pltpu.roll(t, by, 0), pltpu.roll(g[d], by, 0))
            inside = rowz != (0 if d == 5 else nz - 1)
            total = total + jnp.where(inside, got, 0.0)
            new_heat[d, x] = jnp.where(is_pore & inside, got, g[d])
        total = jnp.where(is_pore, total, 0.0)
        temp[x] = total
        zmsg[x] = edge_tile(total[first], total[last], row)
        pairs = [(g[6][first], g[5][last]), ((own - g[6])[first], (own - g[5])[last])]
        for up, down in ZPAIRS:
            pairs.append((flow[down, x, first, :], flow[up, x, last, :]))
        zmsg[nx + x] = pack_pairs(pairs[:4], row)
        zmsg[2 * nx + x] = pack_pairs(pairs[4:], row)
    ends = (hot[2, 0], hot[1, nx - 1], bounce[0], bounce[1])
    for n, v in enumerate(ends):
        zmsg[3 * nx + n] = edge_tile(v[first], v[last], row)
    zmsg[3 * nx + 4 :] = rows_in[...]


def put_plane(out, n, v):
    tiles = v.shape[0] // TILE
    for i in range(tiles):
        out[n + i] = v[i * TILE : (i + 1) * TILE]
    return n + tiles


def get_plane(ref, n, tiles):
    return ref[n : n + tiles].reshape(tiles * TILE, ref.shape[-1])


def early_body(tsm, km, flow, after, low, high):
    nx = tsm.shape[0]
    for side, out in ((0, low), (1, high)):
        n = 0
        for field in (tsm, km):
            for x in range(side * (nx - DEEP), side * (nx - DEEP) + DEEP):
                n = put_plane(out, n, field[x])
        for d in (XLOW, XHIGH)[side]:
            n = put_plane(out, n, flow[d, side * (nx - 1)])


def zjoin_body(mine, theirs, temp, hot, bounce, heat_in, after, heat_ends, low, high):
    nx, nz, ny = temp.shape
    row = rows8((TILE, ny))
    edge = (row == 0) | (row == TILE - 1)
    first, last = slice(0, TILE), slice(nz - TILE, nz)

    def swap(v):
        return jnp.where(row < DEEP, pltpu.roll(v, 1, 0), pltpu.roll(v, TILE - 1, 0))

    def slot1(v):
        return jnp.where(row < DEEP, pltpu.roll(v, TILE - 1, 0), pltpu.roll(v, 1, 0))

    at = [0, 0]
    for x in range(nx):
        my_t, their_t = mine[3 * nx + 4 + x], theirs[3 * nx + 4 + x]
        my_p, their_p = mine[nx + x], theirs[nx + x]
        near = swap(their_t)
        got = jnp.where(near == 0.0, swap(their_p), slot1(my_p) + WALL_NEAR * near)
        mine_in = edge & (my_t == 0.0)
        add = jnp.where(mine_in, got, 0.0)
        near = swap(my_t)
        back = jnp.where(near == 0.0, swap(my_p), slot1(their_p) + WALL_NEAR * near)
        back = jnp.where(edge & (their_t == 0.0), back, 0.0)
        heat_ends[0, x] = jnp.where(mine_in & (row == 0), got, heat_in[5, x, first, :])
        heat_ends[1, x] = jnp.where(mine_in & (row == TILE - 1), got, heat_in[6, x, last, :])
        for side, out in ((0, low), (1, high)):
            if side * (nx - DEEP) <= x < side * (nx - DEEP) + DEEP:
                n = at[side]
                out[n] = temp[x, first, :] + jnp.where(row == 0, add, 0.0)
                n = put_plane(out, n + 1, temp[x, TILE : nz - TILE, :])
                out[n] = temp[x, last, :] + jnp.where(row == TILE - 1, add, 0.0)
                out[n + 1] = theirs[x] + back
                at[side] = n + 2
    for side, out in ((0, low), (1, high)):
        x = side * (nx - 1)
        n = put_plane(out, at[side], hot[2 - side, x])
        out[n] = theirs[3 * nx + side]
        n = put_plane(out, n + 1, bounce[side])
        out[n] = theirs[3 * nx + 2 + side]
        a, b = theirs[nx + x], theirs[2 * nx + x]
        if side:
            out[n + 1] = jnp.where(row < DEEP, b, pltpu.roll(a, 3, 0))
        else:
            out[n + 1] = jnp.where(row < DEEP, pltpu.roll(a, TILE - 3, 0), b)
        for f in range(2):
            base = 3 * nx + 4 + f * nx + side * (nx - DEEP)
            out[n + 2 + f * DEEP : n + 2 + (f + 1) * DEEP] = theirs[base : base + DEEP]


def reader(nx, early, late, fields, rows):
    tiles = fields[0].shape[1] // TILE
    corner = (DEEP + 2) * (tiles + 1) + 1

    def core(f, p):
        if DEEP <= p < DEEP + nx:
            return fields[f][p - DEEP]
        side, n = (0, p) if p < DEEP else (1, p - DEEP - nx)
        return get_plane(early[side], (f * DEEP + n) * tiles, tiles)

    def halo(f, p):
        if DEEP <= p < DEEP + nx:
            return rows[3 * nx + 4 + f * nx + p - DEEP]
        side, n = (0, p) if p < DEEP else (1, p - DEEP - nx)
        return late[side][corner + f * DEEP + n]

    def whole(f, p):
        return jnp.concatenate([core(f, p), halo(f, p)], axis=0)

    return core, halo, whole


def face(a, b):
    return (2.0 * a) * b / jnp.maximum(a + b, 1.0)


def still_plane(whole, p, fx_low, fx_high):
    k, t = whole(1, p), whole(0, p)
    ext, ny = k.shape
    ky = pltpu.roll(k, 1, 1)
    kz = pltpu.roll(k, 1, 0)
    gy, gz = face(k, ky), face(k, kz)
    pore = jnp.where(k == 0.0, 1.0, 0.0)
    count = jnp.where(ky == 0.0, 1.0, 0.0) + jnp.where(kz == 0.0, 1.0, 0.0)
    count = count + pltpu.roll(pore, ny - 1, 1) + pltpu.roll(pore, ext - 1, 0)
    count = count + jnp.where(whole(1, p - 1) == 0.0, 1.0, 0.0) + jnp.where(whole(1, p + 1) == 0.0, 1.0, 0.0)
    flux_y = gy * (pltpu.roll(t, 1, 1) - t)
    flux_z = gz * (pltpu.roll(t, 1, 0) - t)
    net = fx_low * (whole(0, p - 1) - t) - fx_high * (t - whole(0, p + 1))
    net = net + (flux_y - pltpu.roll(flux_y, ny - 1, 1))
    net = net + (flux_z - pltpu.roll(flux_z, ext - 1, 0))
    return gy, gz, net - FILM * count * t


def static_body(tsm, km, theirs, fx, fy, fz, still):
    nx = tsm.shape[0]
    _, _, whole = reader(nx, None, None, (tsm, km), theirs)
    first = DEEP + 1
    for n in range(nx - 1):
        fx[n] = face(whole(1, first + n), whole(1, first + n - 1))
    for n in range(nx - 2):
        fy[n], fz[n], still[n] = still_plane(whole, first + n, fx[n], fx[n + 1])


def conduct_body(*all_refs):
    early_low, early_high, from_low, low, high, from_high, theirs = all_refs[0:7]
    in_fx, in_fy, in_fz, in_still, tsm, km, hot, ts, corners, heat_in, pops_in, new_heat, new_pops, new_solid = all_refs[7:21]
    temp, resid, step_a, step_b, fx, fy, fz, still, ends, patched, sems = all_refs[21:]
    nx, nz, ny = ts.shape
    planes, ext = temp.shape[:2]
    tiles = ext // TILE
    own = slice(0, nz)
    late = (from_low, low, high, from_high)
    core, halo, whole = reader(nx, (early_low, early_high), (from_low, from_high), (tsm, km), theirs)

    def ready(p):
        return DEEP < p < DEEP + nx - 1

    def fx_at(p):
        return in_fx[p - DEEP - 1] if DEEP < p < DEEP + nx else fx[p]

    def fy_at(p):
        return in_fy[p - DEEP - 1] if ready(p) else fy[p]

    def fz_at(p):
        return in_fz[p - DEEP - 1] if ready(p) else fz[p]

    def still_at(p):
        return in_still[p - DEEP - 1] if ready(p) else still[p]

    def ts_at(p):
        return whole(0, p)

    def temp_at(p):
        ref, n = ((from_low, p), (low, p - DEEP), (high, p - nx), (from_high, p - DEEP - nx))[p // DEEP]
        return get_plane(ref, n * tiles, tiles)

    def out_of(ref):
        return get_plane(ref, DEEP * tiles, tiles)

    def bounce_of(ref):
        return get_plane(ref, (DEEP + 1) * tiles, tiles)

    def join(below, above, p_low, p_high):
        t_low, t_high = ts_at(p_low), ts_at(p_high)
        up = jnp.where(t_low == 0.0, out_of(below), bounce_of(above) + WALL_NEAR * t_low)
        down = jnp.where(t_high == 0.0, out_of(above), bounce_of(below) + WALL_NEAR * t_high)
        temp[p_high] = jnp.where(t_high == 0.0, temp_at(p_high) + up, 0.0)
        temp[p_low] = jnp.where(t_low == 0.0, temp_at(p_low) + down, 0.0)
        return up, down

    row = rows8((TILE, ny))
    corner = (DEEP + 2) * tiles
    copies = []
    for n, (d, x, p, ref) in enumerate(
        (
            (11, 0, DEEP - 1, from_low),
            (13, 0, DEEP - 1, from_low),
            (12, nx - 1, DEEP + nx, from_high),
            (14, nx - 1, DEEP + nx, from_high),
        )
    ):
        by, at, rows = (1, 0, slice(0, TILE)) if DIRS[d][2] > 0 else (TILE - 1, TILE - 1, slice(nz - TILE, nz))
        there = pltpu.roll(halo(0, p), by, 0)
        both = (row == at) & (tsm[x, rows, :] == 0.0) & (there == 0.0)
        patched[n] = jnp.where(both, pltpu.roll(ref[corner], by, 0), corners[n])
        copies.append(pltpu.make_async_copy(patched.at[n], new_pops.at[d, x, rows, :], sems.at[n]))
        copies[-1].start()
    for p in range(1, planes - 1):
        if p not in (DEEP - 1, DEEP, DEEP + nx - 1, DEEP + nx):
            temp[p] = temp_at(p)
    temp[0] = temp_at(0)
    temp[planes - 1] = temp_at(planes - 1)
    up, _ = join(from_low, low, DEEP - 1, DEEP)
    _, down = join(high, from_high, DEEP + nx - 1, DEEP + nx)
    ends[0] = jnp.where(tsm[0] == 0.0, up[own], hot[1, 0])
    ends[1] = jnp.where(tsm[nx - 1] == 0.0, down[own], hot[2, nx - 1])
    for n, (d, x) in enumerate(((1, 0), (2, nx - 1))):
        copies.append(pltpu.make_async_copy(ends.at[n], new_heat.at[d, x], sems.at[4 + n]))
        copies[-1].start()

    for p in range(1, planes):
        if not DEEP < p < DEEP + nx:
            fx[p] = face(whole(1, p), whole(1, p - 1))
    for p in range(1, planes - 1):
        if not ready(p):
            fy[p], fz[p], still[p] = still_plane(whole, p, fx_at(p), fx_at(p + 1))
    for p in range(1, planes - 1):
        mid = temp[p]
        near = (temp[p - 1] + temp[p + 1]) + (pltpu.roll(mid, 1, 1) + pltpu.roll(mid, ny - 1, 1))
        near = near + (pltpu.roll(mid, 1, 0) + pltpu.roll(mid, ext - 1, 0))
        r = jnp.where(ts_at(p) == 0.0, 0.0, FILM * near) + still_at(p)
        resid[p] = r
        s = r * (1.0 / THETA)
        step_a[p] = s
        if DEEP <= p < DEEP + nx:
            new_solid[p - DEEP] = ts[p - DEEP] + s[own]
    sigma = THETA / DELTA
    ratio = 1.0 / sigma
    now, later = step_a, step_b
    for sweep in range(1, ITERS):
        after = 1.0 / (2.0 * sigma - ratio)
        start = 1 + sweep
        below = fx_at(start) * (now[start - 1] - now[start])
        for p in range(start, planes - start):
            v = now[p]
            flux_y = fy_at(p) * (pltpu.roll(v, 1, 1) - v)
            flux_z = fz_at(p) * (pltpu.roll(v, 1, 0) - v)
            above = fx_at(p + 1) * (v - now[p + 1])
            net = (below - above) + (flux_y - pltpu.roll(flux_y, ny - 1, 1))
            net = net + (flux_z - pltpu.roll(flux_z, ext - 1, 0))
            below = above
            r = resid[p] - (v - net)
            s = (after * ratio) * v + (2.0 * after / DELTA) * r
            if sweep + 1 < ITERS:
                resid[p] = r
                later[p] = s
            if DEEP <= p < DEEP + nx:
                new_solid[p - DEEP] = new_solid[p - DEEP] + s[own]
        ratio = after
        now, later = later, now
    for copy in copies:
        copy.wait()


FLOW_DIRS = (
    (0, 1, 2, 3, 4, 7, 8, 9, 10),
    (5, 6, 11, 12, 13, 14, 15, 16, 17, 18),
    tuple(range(19)),
)
FLOW_RUNS = (((0, 5), (7, 4)), ((5, 2), (11, 8)), ((0, 19),))


def flow_body(part, *all_refs):
    early = late = theirs = None
    if part == 0:
        flow, tsm, out, done, buf, sems = all_refs
    elif part == 1:
        flow, tsm, theirs, heat, heat_ends, held, out, heat_out, buf, sems, heat_sems = all_refs
    else:
        flow, tsm, theirs, early_low, early_high, held, out, corners, buf, sems = all_refs
        early = (early_low, early_high)
    nx, nz, ny = flow.shape[1:]
    tiles = nz // TILE
    ext = nz + TILE
    rowz = rows8((nz, ny))
    core, _, whole = reader(nx, early, None, (tsm, None), theirs)
    if part == 1:
        copy_heat = pltpu.make_async_copy(heat, heat_out, heat_sems.at[0])
        copy_heat.start()

    def source(d, q):
        if 0 <= q < nx:
            return flow[d, q]
        ref, n = (early_low, XHIGH.index(d)) if q < 0 else (early_high, XLOW.index(d))
        return get_plane(ref, (2 * DEEP + n) * tiles, tiles)

    copies = []
    for at, x in enumerate(range(1, nx - 1) if part < 2 else (0, nx - 1)):
        slot = at % 2
        if at >= 2:
            for copy in copies[at - 2]:
                copy.wait()
        is_pore = tsm[x] == 0.0
        turned = {}
        for at_d, d in enumerate(FLOW_DIRS[part]):
            if d == 0:
                buf[slot, at_d] = flow[0, x]
                continue
            cx, cy, cz = DIRS[d]
            q = x - cx
            inside = 0 <= q < nx
            tall = bool(cz) and inside
            if (cx, cy, tall) not in turned:
                t = (whole if tall else core)(0, q + DEEP)
                turned[cx, cy, tall] = pltpu.roll(t, cy % ny, 1) if cy else t
            t = turned[cx, cy, tall]
            if cz:
                t = pltpu.roll(t, cz % t.shape[0], 0)
            both = is_pore & (t[0:nz] == 0.0)
            v = source(d, q)
            if cz:
                at_end = rowz == (0 if cz > 0 else nz - 1)
                v = pltpu.roll(v, cz % nz, 0)
                if inside:
                    block, j = ZSLOT[d]
                    n = TILE - 1 - j if cz > 0 else j
                    v = jnp.where(at_end, theirs[block * nx + q, n : n + 1, :], v)
                else:
                    both = both & ~at_end
            if cy:
                v = pltpu.roll(v, cy % ny, 1)
            v = jnp.where(both, v, jnp.where(is_pore, flow[OPP[d], x], flow[d, x]))
            buf[slot, at_d] = v
            if cz and not inside:
                corners[(11, 13, 12, 14).index(d)] = v[0:TILE] if cz > 0 else v[nz - TILE : nz]
        begin = 0
        copies.append([])
        for n, (d, count) in enumerate(FLOW_RUNS[part]):
            src, dst = buf.at[slot, begin : begin + count], out.at[d : d + count, x]
            copies[-1].append(pltpu.make_async_copy(src, dst, sems.at[2 * slot + n]))
            copies[-1][-1].start()
            begin += count
    if part == 0:
        done[...] = jnp.zeros(done.shape, jnp.float32)
    if part == 1:
        copy_heat.wait()
        for n, rows in ((0, slice(0, TILE)), (1, slice(nz - TILE, nz))):
            copy = pltpu.make_async_copy(heat_ends.at[n], heat_out.at[5 + n, :, rows, :], heat_sems.at[n])
            copy.start()
            copies[-1].append(copy)
    for group in copies[-2:]:
        for copy in group:
            copy.wait()


def ring(axis, by):
    count = lax.axis_size(axis)
    return [(i, (i + by) % count) for i in range(count)]


def along_z(rows):
    if lax.axis_size("grp") == 2:
        return lax.ppermute(rows, "grp", ring("grp", 1))
    from_below = lax.ppermute(rows, "grp", ring("grp", 1))
    from_above = lax.ppermute(rows, "grp", ring("grp", -1))
    upper = lax.broadcasted_iota(jnp.int32, rows.shape, 1) < DEEP
    return jnp.where(upper, from_above, from_below)


def along_x(low, high):
    return lax.ppermute(high, "dev", ring("dev", 1)), lax.ppermute(low, "dev", ring("dev", -1))


def per_device(populations, heat_pops, solid_temp, conductivity, pore_mask):
    nx, nz, ny = solid_temp.shape
    ext = nz + TILE
    tiles = ext // TILE
    planes = nx + 2 * DEEP
    field = (nx, nz, ny)
    wide = (planes, ext, ny)
    dma = pltpu.SemaphoreType.DMA
    flow, hot, tsm, km, my_rows = call(
        collide_body,
        [(19, *field), (7, *field), field, field, (2 * nx, TILE, ny)],
        [pltpu.with_memory_space_constraint(v, pltpu.HBM) for v in (populations, heat_pops, solid_temp, conductivity, pore_mask)],
        in_specs=[HBM] * 5,
        scratch=[
            pltpu.VMEM((19, *field), jnp.float32),
            pltpu.VMEM((7, *field), jnp.float32),
            pltpu.VMEM(field, jnp.float32),
            pltpu.VMEM(field, jnp.float32),
            pltpu.VMEM(field, jnp.int32),
            dma((3 + 2 * nx,)),
        ],
        limit=12 << 20,
        us=4,
    )
    new_heat, temp, bounce, zmsg = call(
        heat_body,
        [(7, *field), field, (2, nz, ny), (5 * nx + 4, TILE, ny)],
        [hot, flow, tsm, my_rows],
    )
    theirs = along_z(zmsg)
    early_shape = ((2 * DEEP + len(XLOW)) * (tiles - 1), TILE, ny)
    early_low, early_high = call(early_body, [early_shape] * 2, [tsm, km, flow, bounce])
    early_low, early_high = along_x(early_low, early_high)

    def flow_call(part, outs, args, out_specs, in_hbm=0, extra=(), **rest):
        held = (2, len(FLOW_DIRS[part]), nz, ny)
        return call(
            functools.partial(flow_body, part),
            outs,
            args,
            in_specs=[VM] * (len(args) - in_hbm) + [ANY] * in_hbm,
            out_specs=out_specs,
            scratch=[pltpu.VMEM(held, jnp.float32), dma((4,)), *extra],
            limit=6 << 20,
            **rest,
        )

    pops_shape, heat_shape = (19, *field), (7, *field)
    new_pops, after = flow_call(0, [pops_shape, (TILE, 128)], [flow, tsm], [ANY, VM], us=20)
    late_shape = ((DEEP + 2) * tiles + 1 + 2 * DEEP, TILE, ny)
    heat_ends, low, high = call(
        zjoin_body,
        [(2, nx, TILE, ny), late_shape, late_shape],
        [zmsg, theirs, temp, hot, bounce, new_heat, after],
    )
    from_low, from_high = along_x(low, high)
    new_pops, new_heat = flow_call(
        1,
        [pops_shape, heat_shape],
        [flow, tsm, theirs, new_heat, heat_ends, new_pops],
        [ANY, ANY],
        in_hbm=1,
        extra=[dma((2,))],
        aliases={5: 0},
        us=20,
    )
    new_pops, corners = flow_call(
        2,
        [pops_shape, (4, TILE, ny)],
        [flow, tsm, theirs, early_low, early_high, new_pops],
        [ANY, VM],
        in_hbm=1,
        aliases={5: 0},
    )
    fx, fy, fz, still = call(
        static_body,
        [(nx - 1, ext, ny)] + [(nx - 2, ext, ny)] * 3,
        [tsm, km, theirs],
    )
    new_heat, new_pops, new_solid = call(
        conduct_body,
        [heat_shape, pops_shape, field],
        [early_low, early_high, from_low, low, high, from_high, theirs]
        + [fx, fy, fz, still, tsm, km, hot, solid_temp, corners, new_heat, new_pops],
        in_specs=[VM] * 16 + [ANY] * 2,
        out_specs=[ANY, ANY, VM],
        scratch=[pltpu.VMEM(wide, jnp.float32)] * 8
        + [pltpu.VMEM((2, nz, ny), jnp.float32), pltpu.VMEM((4, TILE, ny), jnp.float32), dma((6,))],
        aliases={16: 0, 17: 1},
        limit=10 << 20,
        us=4,
    )
    return new_pops, new_heat, new_solid


def solution(mesh):
    wide = P(None, "dev", "grp", None)
    flat = P("dev", "grp", None)
    return jax.shard_map(
        per_device,
        mesh=mesh,
        in_specs=(wide, wide, flat, flat, flat),
        out_specs=(wide, wide, flat),
        check_vma=False,
    )
```

```python
import functools

import jax
import jax.numpy as jnp
from jax import lax
from jax.experimental import pallas as pl
from jax.experimental.pallas import tpu as pltpu
from jax.sharding import PartitionSpec as P

ITERS = 4
DIRS = (
    (0, 0, 0),
    (1, 0, 0),
    (-1, 0, 0),
    (0, 1, 0),
    (0, -1, 0),
    (0, 0, 1),
    (0, 0, -1),
    (1, 1, 0),
    (-1, -1, 0),
    (1, -1, 0),
    (-1, 1, 0),
    (1, 0, 1),
    (-1, 0, -1),
    (1, 0, -1),
    (-1, 0, 1),
    (0, 1, 1),
    (0, -1, -1),
    (0, 1, -1),
    (0, -1, 1),
)
OPP = (0, 2, 1, 4, 3, 6, 5, 8, 7, 10, 9, 12, 11, 14, 13, 16, 15, 18, 17)
PAIRS = ((1, 2), (3, 4), (5, 6), (7, 8), (9, 10), (11, 12), (13, 14), (15, 16), (17, 18))
ZPAIRS = ((11, 12), (14, 13), (5, 6), (15, 16), (18, 17))
ZSLOT = {11: 2, 12: 2, 14: 3, 13: 3, 5: 0, 6: 0, 15: 1, 16: 1, 18: 2, 17: 2}
XHIGH = (1, 7, 9, 11, 13)
XLOW = (2, 8, 10, 12, 14)
W0, W1, W2 = 1.0 / 3.0, 1.0 / 18.0, 1.0 / 36.0
RELAX_FLOW = 0.8
RELAX_HEAT = 0.7
JUMP = 0.3
FILM = 0.5
THETA = 61.0
DELTA = 60.0
WALL_OWN = 0.25 * JUMP
WALL_NEAR = 0.25 * (1.0 - JUMP)
DEEP = 4
TILE = 8

VM = pl.BlockSpec(memory_space=pltpu.VMEM)
ANY = pl.BlockSpec(memory_space=pl.ANY)
HBM = pl.BlockSpec(memory_space=pltpu.HBM)


def call(body, outs, args, in_specs=None, out_specs=None, scratch=(), aliases=None, limit=4 << 20, us=0.5):
    return pl.pallas_call(
        body,
        out_shape=[jax.ShapeDtypeStruct(shape, jnp.float32) for shape in outs],
        in_specs=in_specs or [VM] * len(args),
        out_specs=out_specs or [VM] * len(outs),
        scratch_shapes=list(scratch),
        input_output_aliases=aliases or {},
        compiler_params=pltpu.CompilerParams(vmem_limit_bytes=limit),
        cost_estimate=pl.CostEstimate(flops=int(us * 1e9), bytes_accessed=int(us * 3e6), transcendentals=0),
    )(*args)


def rows8(shape):
    return lax.broadcasted_iota(jnp.int32, shape, 0)


def collide_body(*refs):
    sources, (flow, hot, tsm, km, rows_out), held, sems = refs[:5], refs[5:10], refs[10:15], refs[15]
    pops, heat, ts, cond, pore = held
    nx, nz, ny = tsm.shape
    row = rows8((TILE, ny))

    def fetch(n, x):
        if n < 2:
            return pltpu.make_async_copy(sources[n].at[:, x], held[n].at[:, x], sems.at[3 + n * nx + x])
        return pltpu.make_async_copy(sources[n], held[n], sems.at[n - 2])

    for n in (2, 3, 4):
        fetch(n, 0).start()
    for x in range(nx):
        for n in (0, 1):
            fetch(n, x).start()
    for n in (2, 3, 4):
        fetch(n, 0).wait()

    def plane(x, carry):
        is_pore = pore[x] != 0
        for n, (src, dst) in enumerate(((ts, tsm), (cond, km))):
            v = jnp.where(is_pore, 0.0, src[x])
            dst[x] = v
            if n:
                rows_out[x] = edge_tile(v[0:TILE], v[nz - TILE : nz], row)
        for n in (0, 1):
            fetch(n, x).wait()
        return lax.fori_loop(0, nz // TILE, lambda i, c: step(x, i, c), carry)

    def step(x, i, carry):
        rows = pl.ds(pl.multiple_of(i * TILE, TILE), TILE)
        is_pore = tsm[x, rows, :] == 0.0
        p = [pops[d, x, rows, :] for d in range(19)]
        diff = [p[a] - p[b] for a, b in PAIRS]
        rho = p[0]
        for a, b in PAIRS:
            rho = rho + (p[a] + p[b])
        inv = 1.0 / rho
        ux = (diff[0] + diff[3] + diff[4] + diff[5] + diff[6]) * inv
        uy = (diff[1] + diff[3] - diff[4] + diff[7] + diff[8]) * inv
        uz = (diff[2] + diff[5] - diff[6] + diff[7] - diff[8]) * inv
        base = 1.0 - 1.5 * (ux * ux + uy * uy + uz * uz)
        keep = 1.0 - 1.0 / RELAX_FLOW
        flow[0, x, rows, :] = jnp.where(is_pore, (W0 / RELAX_FLOW) * rho * base + keep * p[0], p[0])
        speeds = (ux, uy, uz, ux + uy, ux - uy, ux + uz, ux - uz, uy + uz, uy - uz)
        scaled1 = (W1 / RELAX_FLOW) * rho
        scaled2 = (W2 / RELAX_FLOW) * rho
        for n, (a, b) in enumerate(PAIRS):
            scaled = scaled1 if n < 3 else scaled2
            cu = speeds[n]
            even = scaled * (base + 4.5 * (cu * cu))
            odd = scaled * (3.0 * cu)
            flow[a, x, rows, :] = jnp.where(is_pore, (even + odd) + keep * p[a], p[a])
            flow[b, x, rows, :] = jnp.where(is_pore, (even - odd) + keep * p[b], p[b])
        h = [heat[d, x, rows, :] for d in range(7)]
        temp = h[0] + (h[1] + h[2]) + (h[3] + h[4]) + (h[5] + h[6])
        hkeep = 1.0 - 1.0 / RELAX_HEAT
        hot[0, x, rows, :] = jnp.where(is_pore, (0.25 / RELAX_HEAT) * temp + hkeep * h[0], h[0])
        even = (0.125 / RELAX_HEAT) * temp
        for n in range(3):
            a, b = PAIRS[n]
            odd = even * (4.0 * speeds[n])
            hot[a, x, rows, :] = jnp.where(is_pore, (even + odd) + hkeep * h[a], h[a])
            hot[b, x, rows, :] = jnp.where(is_pore, (even - odd) + hkeep * h[b], h[b])
        return carry

    lax.fori_loop(0, nx, plane, 0)


def edge_tile(low, high, row):
    return jnp.where(row < DEEP, low, high)


def pack_pairs(pairs, row):
    out = None
    for j, (low, high) in enumerate(pairs):
        if j:
            low, high = pltpu.roll(low, j, 0), pltpu.roll(high, TILE - j, 0)
        both = jnp.where(row < DEEP, low, high)
        out = both if out is None else jnp.where((row == j) | (row == TILE - 1 - j), both, out)
    return out


def heat_body(hot, flow, tsm, rows_in, new_heat, temp, bounce, zmsg, zflow):
    nx, nz, ny = tsm.shape
    rowz = rows8((nz, ny))
    row = rows8((TILE, ny))
    first, last = slice(0, TILE), slice(nz - TILE, nz)
    for x in range(nx):
        t = tsm[x]
        is_pore = t == 0.0
        g = [hot[d, x] for d in range(7)]
        own = WALL_OWN * (g[0] + (g[1] + g[2]) + (g[3] + g[4]) + (g[5] + g[6]))
        new_heat[0, x] = g[0]
        total = g[0]

        def arrive(d, near, moved):
            return jnp.where(near == 0.0, moved, (own - g[OPP[d]]) + WALL_NEAR * near)

        for d in (1, 2):
            src = x - DIRS[d][0]
            if 0 <= src < nx:
                got = arrive(d, tsm[src], hot[d, src])
                total = total + got
                new_heat[d, x] = jnp.where(is_pore, got, g[d])
            else:
                new_heat[d, x] = g[d]
                bounce[0 if x == 0 else 1] = own - g[OPP[d]]
        for d in (3, 4):
            by = DIRS[d][1] % ny
            got = arrive(d, pltpu.roll(t, by, 1), pltpu.roll(g[d], by, 1))
            total = total + got
            new_heat[d, x] = jnp.where(is_pore, got, g[d])
        for d in (5, 6):
            by = DIRS[d][2] % nz
            got = arrive(d, pltpu.roll(t, by, 0), pltpu.roll(g[d], by, 0))
            inside = rowz != (0 if d == 5 else nz - 1)
            total = total + jnp.where(inside, got, 0.0)
            new_heat[d, x] = jnp.where(is_pore & inside, got, g[d])
        total = jnp.where(is_pore, total, t)
        temp[x] = total
        zmsg[x] = edge_tile(total[first], total[last], row)
        pairs = [(g[6][first], g[5][last]), ((own - g[6])[first], (own - g[5])[last])]
        for up, down in ZPAIRS:
            pairs.append((flow[down, x, first, :], flow[up, x, last, :]))
        zmsg[nx + x] = pack_pairs(pairs[:4], row)
        zflow[x] = pack_pairs(pairs[4:], row)
    ends = (hot[2, 0], hot[1, nx - 1], bounce[0], bounce[1])
    for n, v in enumerate(ends):
        zmsg[2 * nx + n] = edge_tile(v[first], v[last], row)
    zmsg[2 * nx + 4 :] = rows_in[...]


def put_plane(out, n, v):
    tiles = v.shape[0] // TILE
    for i in range(tiles):
        out[n + i] = v[i * TILE : (i + 1) * TILE]
    return n + tiles


def get_plane(ref, n, tiles):
    return ref[n : n + tiles].reshape(tiles * TILE, ref.shape[-1])


def parity():
    return lax.axis_index("dev") % 2


def by_side(cross, intra, body):
    odd = parity()
    for value, (low, high) in enumerate(((cross, intra), (intra, cross))):

        @pl.when(odd == value)
        def _(low=low, high=high):
            body(low, high)


def picker(cross, intra):
    odd = parity()

    def pick(side, n, tiles):
        across, within = get_plane(cross, n, tiles), get_plane(intra, n, tiles)
        even_value, odd_value = (across, within) if side == 0 else (within, across)
        return jnp.where(jnp.full(across.shape, odd) == 0, even_value, odd_value)

    return pick


def early_body(km, flow, hot, bounce, temp, cross, intra):
    nx, nz = km.shape[:2]

    def fill(low, high):
        for side, out in ((0, low), (1, high)):
            n = 0
            deep = range(side * (nx - DEEP), side * (nx - DEEP) + DEEP)
            for x in deep:
                n = put_plane(out, n, km[x])
            for d in (XLOW, XHIGH)[side]:
                n = put_plane(out, n, flow[d, side * (nx - 1)])
            n = put_plane(out, n, hot[2 - side, side * (nx - 1)])
            n = put_plane(out, n, bounce[side])
            for x in deep:
                n = put_plane(out, n, temp[x, TILE : nz - TILE, :])

    by_side(cross, intra, fill)


def zjoin_body(mine, theirs, temp, heat_in, after, heat_ends, joined, cross, intra):
    nx, nz, ny = temp.shape
    row = rows8((TILE, ny))
    edge = (row == 0) | (row == TILE - 1)
    first, last = slice(0, TILE), slice(nz - TILE, nz)

    def swap(v):
        return jnp.where(row < DEEP, pltpu.roll(v, 1, 0), pltpu.roll(v, TILE - 1, 0))

    def slot1(v):
        return jnp.where(row < DEEP, pltpu.roll(v, TILE - 1, 0), pltpu.roll(v, 1, 0))

    for x in range(nx):
        my_k, their_k = mine[2 * nx + 4 + x], theirs[2 * nx + 4 + x]
        my_t, their_t = jnp.where(my_k == 0.0, 0.0, mine[x]), jnp.where(their_k == 0.0, 0.0, theirs[x])
        my_p, their_p = mine[nx + x], theirs[nx + x]
        near = swap(their_t)
        got = jnp.where(near == 0.0, swap(their_p), slot1(my_p) + WALL_NEAR * near)
        mine_in = edge & (my_t == 0.0)
        add = jnp.where(mine_in, got, 0.0)
        near = swap(my_t)
        back = jnp.where(near == 0.0, swap(my_p), slot1(their_p) + WALL_NEAR * near)
        back = jnp.where(edge & (their_t == 0.0), back, 0.0)
        heat_ends[0, x] = jnp.where(mine_in & (row == 0), got, heat_in[5, x, first, :])
        heat_ends[1, x] = jnp.where(mine_in & (row == TILE - 1), got, heat_in[6, x, last, :])
        joined[x, first, :] = temp[x, first, :] + jnp.where(row == 0, add, 0.0)
        joined[x, TILE : nz - TILE, :] = temp[x, TILE : nz - TILE, :]
        joined[x, last, :] = temp[x, last, :] + jnp.where(row == TILE - 1, add, 0.0)
        joined[x, nz : nz + TILE, :] = theirs[x] + back

    def fill(low, high):
        for side, out in ((0, low), (1, high)):
            for n in range(DEEP):
                v = joined.at[side * (nx - DEEP) + n]
                out[3 * n] = v[first, :]
                out[3 * n + 1] = v[last, :]
                out[3 * n + 2] = v[nz : nz + TILE, :]
            n = 3 * DEEP
            out[n] = theirs[2 * nx + side]
            out[n + 1] = theirs[2 * nx + 2 + side]
            v = theirs[nx + side * (nx - 1)]
            lower, upper = (5, 2) if side else (6, 3)
            out[n + 2] = jnp.where(row < DEEP, pltpu.roll(v, lower, 0), pltpu.roll(v, upper, 0))
            base = 2 * nx + 4 + side * (nx - DEEP)
            out[n + 3 : n + 3 + DEEP] = theirs[base : base + DEEP]

    by_side(cross, intra, fill)


def reader(nx, early, late, tsm, km, rows):
    tiles = km.shape[1] // TILE
    ahead = (DEEP + len(XLOW)) * tiles
    corner = 3 * DEEP + 3

    def away(p):
        return (0, p) if p < DEEP else (1, p - DEEP - nx)

    def km_halo(p):
        if DEEP <= p < DEEP + nx:
            return rows[2 * nx + 4 + p - DEEP]
        side, n = away(p)
        return late(side, corner + n, 1)

    def km_at(p):
        if DEEP <= p < DEEP + nx:
            core = km[p - DEEP]
        else:
            side, n = away(p)
            core = early(side, n * tiles, tiles)
        return jnp.concatenate([core, km_halo(p)], axis=0)

    def temp_far(p):
        side, n = away(p)
        middle = early(side, ahead + 2 * tiles + n * (tiles - 2), tiles - 2)
        ends = late(side, 3 * n, 3)
        return jnp.concatenate([ends[0:TILE], middle, ends[TILE:]], axis=0)

    def ts_at(p):
        if DEEP <= p < DEEP + nx:
            halo = jnp.where(km_halo(p) == 0.0, 0.0, rows[p - DEEP])
            return jnp.concatenate([tsm[p - DEEP], halo], axis=0)
        return jnp.where(km_at(p) == 0.0, 0.0, temp_far(p))

    return ts_at, km_at, km_halo, temp_far, ahead


def face(a, b):
    return (2.0 * a) * b / jnp.maximum(a + b, 1.0)


def still_plane(ts_at, km_at, p, fx_low, fx_high):
    k, t = km_at(p), ts_at(p)
    ext, ny = k.shape
    ky = pltpu.roll(k, 1, 1)
    kz = pltpu.roll(k, 1, 0)
    gy, gz = face(k, ky), face(k, kz)
    pore = jnp.where(k == 0.0, 1.0, 0.0)
    count = jnp.where(ky == 0.0, 1.0, 0.0) + jnp.where(kz == 0.0, 1.0, 0.0)
    count = count + pltpu.roll(pore, ny - 1, 1) + pltpu.roll(pore, ext - 1, 0)
    count = count + jnp.where(km_at(p - 1) == 0.0, 1.0, 0.0) + jnp.where(km_at(p + 1) == 0.0, 1.0, 0.0)
    flux_y = gy * (pltpu.roll(t, 1, 1) - t)
    flux_z = gz * (pltpu.roll(t, 1, 0) - t)
    net = fx_low * (ts_at(p - 1) - t) - fx_high * (t - ts_at(p + 1))
    net = net + (flux_y - pltpu.roll(flux_y, ny - 1, 1))
    net = net + (flux_z - pltpu.roll(flux_z, ext - 1, 0))
    return gy, gz, net - FILM * count * t


def static_body(tsm, km, theirs, fx, fy, fz, still):
    nx = tsm.shape[0]
    ts_at, km_at = reader(nx, None, None, tsm, km, theirs)[:2]
    first = DEEP + 1
    for n in range(nx - 1):
        fx[n] = face(km_at(first + n), km_at(first + n - 1))
    for n in range(nx - 2):
        fy[n], fz[n], still[n] = still_plane(ts_at, km_at, first + n, fx[n], fx[n + 1])


def conduct_body(*all_refs):
    early_cross, early_intra, late_cross, late_intra, theirs, joined, bounce = all_refs[0:7]
    in_fx, in_fy, in_fz, in_still, tsm, km, hot, ts, corners, heat_in, pops_in, new_heat, new_pops, new_solid = all_refs[7:21]
    temp, resid, step_a, step_b, fx, fy, fz, still, ends, patched, sems = all_refs[21:]
    nx, nz, ny = ts.shape
    planes, ext = temp.shape[:2]
    tiles = nz // TILE
    own = slice(0, nz)
    early, late = picker(early_cross, early_intra), picker(late_cross, late_intra)
    ts_at, km_at, km_halo, temp_far, ahead = reader(nx, early, late, tsm, km, theirs)

    def ready(p):
        return DEEP < p < DEEP + nx - 1

    def fx_at(p):
        return in_fx[p - DEEP - 1] if DEEP < p < DEEP + nx else fx[p]

    def fy_at(p):
        return in_fy[p - DEEP - 1] if ready(p) else fy[p]

    def fz_at(p):
        return in_fz[p - DEEP - 1] if ready(p) else fz[p]

    def still_at(p):
        return in_still[p - DEEP - 1] if ready(p) else still[p]

    def temp_at(p):
        return joined[p - DEEP] if DEEP <= p < DEEP + nx else temp_far(p)

    def sent(n, side):
        return jnp.concatenate([early(side, ahead + n * tiles, tiles), late(side, 3 * DEEP + n, 1)], axis=0)

    def mine(n, side):
        end = (hot[2 - side, side * (nx - 1)], bounce[side])[n]
        return jnp.concatenate([end, theirs[2 * nx + 2 * n + side]], axis=0)

    def join(side):
        p_own = DEEP + side * (nx - 1)
        p_far = p_own - 1 + 2 * side
        t_own, t_far = ts_at(p_own), ts_at(p_far)
        got = jnp.where(t_far == 0.0, sent(0, side), mine(1, side) + WALL_NEAR * t_far)
        back = jnp.where(t_own == 0.0, mine(0, side), sent(1, side) + WALL_NEAR * t_own)
        temp[p_own] = jnp.where(t_own == 0.0, temp_at(p_own) + got, 0.0)
        temp[p_far] = jnp.where(t_far == 0.0, temp_at(p_far) + back, 0.0)
        return got

    row = rows8((TILE, ny))
    corner = 3 * DEEP + 2
    copies = []
    for n, (d, x, p, side) in enumerate(
        (
            (11, 0, DEEP - 1, 0),
            (13, 0, DEEP - 1, 0),
            (12, nx - 1, DEEP + nx, 1),
            (14, nx - 1, DEEP + nx, 1),
        )
    ):
        by, at, rows = (1, 0, slice(0, TILE)) if DIRS[d][2] > 0 else (TILE - 1, TILE - 1, slice(nz - TILE, nz))
        there = pltpu.roll(km_halo(p), by, 0)
        both = (row == at) & (tsm[x, rows, :] == 0.0) & (there == 0.0)
        patched[n] = jnp.where(both, pltpu.roll(late(side, corner, 1), by, 0), corners[n])
        copies.append(pltpu.make_async_copy(patched.at[n], new_pops.at[d, x, rows, :], sems.at[n]))
        copies[-1].start()
    for p in range(planes):
        if p not in (DEEP - 1, DEEP, DEEP + nx - 1, DEEP + nx):
            temp[p] = jnp.where(km_at(p) == 0.0, temp_at(p), 0.0)
    up, down = join(0), join(1)
    ends[0] = jnp.where(tsm[0] == 0.0, up[own], hot[1, 0])
    ends[1] = jnp.where(tsm[nx - 1] == 0.0, down[own], hot[2, nx - 1])
    for n, (d, x) in enumerate(((1, 0), (2, nx - 1))):
        copies.append(pltpu.make_async_copy(ends.at[n], new_heat.at[d, x], sems.at[4 + n]))
        copies[-1].start()

    for p in range(1, planes):
        if not DEEP < p < DEEP + nx:
            fx[p] = face(km_at(p), km_at(p - 1))
    for p in range(1, planes - 1):
        if not ready(p):
            fy[p], fz[p], still[p] = still_plane(ts_at, km_at, p, fx_at(p), fx_at(p + 1))
    for p in range(1, planes - 1):
        mid = temp[p]
        near = (temp[p - 1] + temp[p + 1]) + (pltpu.roll(mid, 1, 1) + pltpu.roll(mid, ny - 1, 1))
        near = near + (pltpu.roll(mid, 1, 0) + pltpu.roll(mid, ext - 1, 0))
        r = jnp.where(km_at(p) == 0.0, 0.0, FILM * near) + still_at(p)
        resid[p] = r
        s = r * (1.0 / THETA)
        step_a[p] = s
        if DEEP <= p < DEEP + nx:
            new_solid[p - DEEP] = ts[p - DEEP] + s[own]
    sigma = THETA / DELTA
    ratio = 1.0 / sigma
    now, later = step_a, step_b
    for sweep in range(1, ITERS):
        after = 1.0 / (2.0 * sigma - ratio)
        start = 1 + sweep
        below = fx_at(start) * (now[start - 1] - now[start])
        for p in range(start, planes - start):
            v = now[p]
            flux_y = fy_at(p) * (pltpu.roll(v, 1, 1) - v)
            flux_z = fz_at(p) * (pltpu.roll(v, 1, 0) - v)
            above = fx_at(p + 1) * (v - now[p + 1])
            net = (below - above) + (flux_y - pltpu.roll(flux_y, ny - 1, 1))
            net = net + (flux_z - pltpu.roll(flux_z, ext - 1, 0))
            below = above
            r = resid[p] - (v - net)
            s = (after * ratio) * v + (2.0 * after / DELTA) * r
            if sweep + 1 < ITERS:
                resid[p] = r
                later[p] = s
            if DEEP <= p < DEEP + nx:
                new_solid[p - DEEP] = new_solid[p - DEEP] + s[own]
        ratio = after
        now, later = later, now
    for copy in copies:
        copy.wait()


FLOW_DIRS = (
    (0, 1, 2, 3, 4, 7, 8, 9, 10),
    (5, 6, 11, 12, 13, 14, 15, 16, 17, 18),
    tuple(range(19)),
)
FLOW_RUNS = (((0, 5), (7, 4)), ((5, 2), (11, 8)), ((0, 19),))


def flow_body(part, *all_refs):
    early = theirs = None
    if part == 0:
        flow, tsm, out, turned, buf, sems = all_refs
    elif part == 1:
        flow, tsm, theirs, flow_rows, turned, heat, heat_ends, held, out, heat_out, buf, sems, heat_sems = all_refs
    else:
        flow, tsm, theirs, flow_rows, turned, early_cross, early_intra, held, out, corners, buf, sems = all_refs
        early = picker(early_cross, early_intra)
    nx, nz, ny = flow.shape[1:]
    tiles = nz // TILE
    row = rows8((TILE, ny))
    if part == 0:
        for x in range(nx):
            for n, by in enumerate((1, ny - 1)):
                turned[n, x] = pltpu.roll(tsm[x], by, 1)
    if part == 1:
        copy_heat = pltpu.make_async_copy(heat, heat_out, heat_sems.at[0])
        copy_heat.start()

    def span(i):
        return slice(i * TILE, (i + 1) * TILE)

    def turn(v, cy):
        return pltpu.roll(v, cy % ny, 1) if cy else v

    def shift(tile, i, cz):
        if not cz:
            return tile(i)
        far, by = (0, 1) if cz > 0 else (TILE - 1, TILE - 1)
        return jnp.where(row == far, pltpu.roll(tile(i - cz), by, 0), pltpu.roll(tile(i), by, 0))

    def mask_tile(q, cy, i):
        if not 0 <= q < nx:
            return turn(early(int(q > 0), (0 if q > 0 else DEEP - 1) * tiles + i % tiles, 1), cy)
        if not 0 <= i < tiles:
            return turn(theirs[2 * nx + 4 + q], cy)
        if cy:
            return turned[0 if cy > 0 else 1, q, span(i), :]
        return tsm[q, span(i), :]

    def flow_tile(d, q, i):
        if 0 <= q < nx:
            if 0 <= i < tiles:
                return flow[d, q, span(i), :]
            v = theirs[nx + q] if d in (11, 12, 13, 14) else flow_rows[q]
            by = ZSLOT[d] if DIRS[d][2] > 0 else TILE - ZSLOT[d]
            return pltpu.roll(v, by % TILE, 0) if by % TILE else v
        side, n = (0, XHIGH.index(d)) if q < 0 else (1, XLOW.index(d))
        return early(side, (DEEP + n) * tiles + i % tiles, 1)

    copies = []
    for at, x in enumerate(range(1, nx - 1) if part < 2 else (0, nx - 1)):
        slot = at % 2
        if at >= 2:
            for copy in copies[at - 2]:
                copy.wait()
        for i in range(tiles):
            is_pore = tsm[x, span(i), :] == 0.0
            for at_d, d in enumerate(FLOW_DIRS[part]):
                if d == 0:
                    buf[slot, at_d, span(i), :] = flow[0, x, span(i), :]
                    continue
                cx, cy, cz = DIRS[d]
                q = x - cx
                t = shift(lambda n: mask_tile(q, cy, n), i, cz)
                both = is_pore & (t == 0.0)
                v = turn(shift(lambda n: flow_tile(d, q, n), i, cz), cy)
                open_row = cz and not 0 <= q < nx and i == (0 if cz > 0 else tiles - 1)
                if open_row:
                    both = both & (row != (0 if cz > 0 else TILE - 1))
                v = jnp.where(both, v, jnp.where(is_pore, flow[OPP[d], x, span(i), :], flow[d, x, span(i), :]))
                buf[slot, at_d, span(i), :] = v
                if open_row:
                    corners[(11, 13, 12, 14).index(d)] = v
        begin = 0
        copies.append([])
        for n, (d, count) in enumerate(FLOW_RUNS[part]):
            src, dst = buf.at[slot, begin : begin + count], out.at[d : d + count, x]
            copies[-1].append(pltpu.make_async_copy(src, dst, sems.at[2 * slot + n]))
            copies[-1][-1].start()
            begin += count
    if part == 1:
        copy_heat.wait()
        for n, rows in ((0, slice(0, TILE)), (1, slice(nz - TILE, nz))):
            copy = pltpu.make_async_copy(heat_ends.at[n], heat_out.at[5 + n, :, rows, :], heat_sems.at[n])
            copy.start()
            copies[-1].append(copy)
    for group in copies[-2:]:
        for copy in group:
            copy.wait()


def ring(axis, by):
    count = lax.axis_size(axis)
    return [(i, (i + by) % count) for i in range(count)]


def along_z(rows):
    if lax.axis_size("grp") == 2:
        return lax.ppermute(rows, "grp", ring("grp", 1))
    from_below = lax.ppermute(rows, "grp", ring("grp", 1))
    from_above = lax.ppermute(rows, "grp", ring("grp", -1))
    upper = lax.broadcasted_iota(jnp.int32, rows.shape, 1) < DEEP
    return jnp.where(upper, from_above, from_below)


def along_x(cross, intra):
    count = lax.axis_size("dev")
    across = [(i, (i + 2 * (i % 2) - 1) % count) for i in range(count)]
    return lax.ppermute(cross, "dev", across), lax.ppermute(intra, "dev", [(i, i ^ 1) for i in range(count)])


def per_device(populations, heat_pops, solid_temp, conductivity, pore_mask):
    nx, nz, ny = solid_temp.shape
    ext = nz + TILE
    tiles = ext // TILE
    planes = nx + 2 * DEEP
    field = (nx, nz, ny)
    wide = (planes, ext, ny)
    dma = pltpu.SemaphoreType.DMA
    flow, hot, tsm, km, my_rows = call(
        collide_body,
        [(19, *field), (7, *field), field, field, (nx, TILE, ny)],
        [pltpu.with_memory_space_constraint(v, pltpu.HBM) for v in (populations, heat_pops, solid_temp, conductivity, pore_mask)],
        in_specs=[HBM] * 5,
        scratch=[
            pltpu.VMEM((19, *field), jnp.float32),
            pltpu.VMEM((7, *field), jnp.float32),
            pltpu.VMEM(field, jnp.float32),
            pltpu.VMEM(field, jnp.float32),
            pltpu.VMEM(field, jnp.int32),
            dma((3 + 2 * nx,)),
        ],
        limit=12 << 20,
        us=4,
    )
    new_heat, temp, bounce, zmsg, zflow = call(
        heat_body,
        [(7, *field), field, (2, nz, ny), (3 * nx + 4, TILE, ny), (nx, TILE, ny)],
        [hot, flow, tsm, my_rows],
    )
    theirs = along_z(zmsg)
    flow_rows = along_z(zflow)
    early_shape = ((DEEP + len(XLOW) + 2) * (tiles - 1) + DEEP * (tiles - 3), TILE, ny)
    early = along_x(*call(early_body, [early_shape] * 2, [km, flow, hot, bounce, temp]))

    def flow_call(part, outs, args, out_specs, in_hbm=0, extra=(), **rest):
        held = (2, len(FLOW_DIRS[part]), nz, ny)
        return call(
            functools.partial(flow_body, part),
            outs,
            args,
            in_specs=[VM] * (len(args) - in_hbm) + [ANY] * in_hbm,
            out_specs=out_specs,
            scratch=[pltpu.VMEM(held, jnp.float32), dma((4,)), *extra],
            limit=6 << 20,
            **rest,
        )

    pops_shape, heat_shape = (19, *field), (7, *field)
    new_pops, turned = flow_call(0, [pops_shape, (2, *field)], [flow, tsm], [ANY, VM], us=20)
    late_shape = (4 * DEEP + 3, TILE, ny)
    heat_ends, joined, cross, intra = call(
        zjoin_body,
        [(2, nx, TILE, ny), (nx, ext, ny), late_shape, late_shape],
        [zmsg, theirs, temp, new_heat, turned],
        us=50,
    )
    late = along_x(cross, intra)
    new_pops, new_heat = flow_call(
        1,
        [pops_shape, heat_shape],
        [flow, tsm, theirs, flow_rows, turned, new_heat, heat_ends, new_pops],
        [ANY, ANY],
        in_hbm=1,
        extra=[dma((2,))],
        aliases={7: 0},
        us=20,
    )
    new_pops, corners = flow_call(
        2,
        [pops_shape, (4, TILE, ny)],
        [flow, tsm, theirs, flow_rows, turned, *early, new_pops],
        [ANY, VM],
        in_hbm=1,
        aliases={7: 0},
    )
    fx, fy, fz, still = call(
        static_body,
        [(nx - 1, ext, ny)] + [(nx - 2, ext, ny)] * 3,
        [tsm, km, theirs],
    )
    new_heat, new_pops, new_solid = call(
        conduct_body,
        [heat_shape, pops_shape, field],
        [*early, *late, theirs, joined, bounce]
        + [fx, fy, fz, still, tsm, km, hot, solid_temp, corners, new_heat, new_pops],
        in_specs=[VM] * 16 + [ANY] * 2,
        out_specs=[ANY, ANY, VM],
        scratch=[pltpu.VMEM(wide, jnp.float32)] * 8
        + [pltpu.VMEM((2, nz, ny), jnp.float32), pltpu.VMEM((4, TILE, ny), jnp.float32), dma((6,))],
        aliases={16: 0, 17: 1},
        limit=10 << 20,
        us=4,
    )
    return new_pops, new_heat, new_solid


def solution(mesh):
    wide = P(None, "dev", "grp", None)
    flat = P("dev", "grp", None)
    return jax.shard_map(
        per_device,
        mesh=mesh,
        in_specs=(wide, wide, flat, flat, flat),
        out_specs=(wide, wide, flat),
        check_vma=False,
    )
```

```python
import functools

import jax
import jax.numpy as jnp
from jax import lax
from jax.experimental import pallas as pl
from jax.experimental.pallas import tpu as pltpu
from jax.sharding import PartitionSpec as P

ITERS = 4
DIRS = (
    (0, 0, 0),
    (1, 0, 0),
    (-1, 0, 0),
    (0, 1, 0),
    (0, -1, 0),
    (0, 0, 1),
    (0, 0, -1),
    (1, 1, 0),
    (-1, -1, 0),
    (1, -1, 0),
    (-1, 1, 0),
    (1, 0, 1),
    (-1, 0, -1),
    (1, 0, -1),
    (-1, 0, 1),
    (0, 1, 1),
    (0, -1, -1),
    (0, 1, -1),
    (0, -1, 1),
)
OPP = (0, 2, 1, 4, 3, 6, 5, 8, 7, 10, 9, 12, 11, 14, 13, 16, 15, 18, 17)
PAIRS = ((1, 2), (3, 4), (5, 6), (7, 8), (9, 10), (11, 12), (13, 14), (15, 16), (17, 18))
ZPAIRS = ((11, 12), (14, 13), (5, 6), (15, 16), (18, 17))
ZSLOT = {11: 2, 12: 2, 14: 3, 13: 3, 5: 0, 6: 0, 15: 1, 16: 1, 18: 2, 17: 2}
XHIGH = (1, 7, 9, 11, 13)
XLOW = (2, 8, 10, 12, 14)
W0, W1, W2 = 1.0 / 3.0, 1.0 / 18.0, 1.0 / 36.0
RELAX_FLOW = 0.8
RELAX_HEAT = 0.7
JUMP = 0.3
FILM = 0.5
THETA = 61.0
DELTA = 60.0
WALL_OWN = 0.25 * JUMP
WALL_NEAR = 0.25 * (1.0 - JUMP)
DEEP = 4
TILE = 8

VM = pl.BlockSpec(memory_space=pltpu.VMEM)
ANY = pl.BlockSpec(memory_space=pl.ANY)
HBM = pl.BlockSpec(memory_space=pltpu.HBM)


def call(body, outs, args, in_specs=None, out_specs=None, scratch=(), aliases=None, limit=4 << 20, us=0.5):
    return pl.pallas_call(
        body,
        out_shape=[jax.ShapeDtypeStruct(shape, jnp.float32) for shape in outs],
        in_specs=in_specs or [VM] * len(args),
        out_specs=out_specs or [VM] * len(outs),
        scratch_shapes=list(scratch),
        input_output_aliases=aliases or {},
        compiler_params=pltpu.CompilerParams(vmem_limit_bytes=limit),
        cost_estimate=pl.CostEstimate(flops=int(us * 1e9), bytes_accessed=int(us * 3e6), transcendentals=0),
    )(*args)


def rows8(shape):
    return lax.broadcasted_iota(jnp.int32, shape, 0)


def collide_body(*refs):
    sources, (flow, hot, tsm, km, rows_out), held, sems = refs[:5], refs[5:10], refs[10:15], refs[15]
    pops, heat, ts, cond, pore = held
    nx, nz, ny = tsm.shape
    row = rows8((TILE, ny))

    def fetch(n, x):
        if n < 2:
            return pltpu.make_async_copy(sources[n].at[:, x], held[n].at[:, x], sems.at[3 + n * nx + x])
        return pltpu.make_async_copy(sources[n], held[n], sems.at[n - 2])

    for n in (2, 3, 4):
        fetch(n, 0).start()
    for x in range(nx):
        for n in (0, 1):
            fetch(n, x).start()
    for n in (2, 3, 4):
        fetch(n, 0).wait()

    def plane(x, carry):
        is_pore = pore[x] != 0
        for n, (src, dst) in enumerate(((ts, tsm), (cond, km))):
            v = jnp.where(is_pore, 0.0, src[x])
            dst[x] = v
            if n:
                rows_out[x] = edge_tile(v[0:TILE], v[nz - TILE : nz], row)
        for n in (0, 1):
            fetch(n, x).wait()
        return lax.fori_loop(0, nz // TILE, lambda i, c: step(x, i, c), carry)

    def step(x, i, carry):
        rows = pl.ds(pl.multiple_of(i * TILE, TILE), TILE)
        is_pore = tsm[x, rows, :] == 0.0
        p = [pops[d, x, rows, :] for d in range(19)]
        diff = [p[a] - p[b] for a, b in PAIRS]
        rho = p[0]
        for a, b in PAIRS:
            rho = rho + (p[a] + p[b])
        inv = 1.0 / rho
        ux = (diff[0] + diff[3] + diff[4] + diff[5] + diff[6]) * inv
        uy = (diff[1] + diff[3] - diff[4] + diff[7] + diff[8]) * inv
        uz = (diff[2] + diff[5] - diff[6] + diff[7] - diff[8]) * inv
        base = 1.0 - 1.5 * (ux * ux + uy * uy + uz * uz)
        keep = 1.0 - 1.0 / RELAX_FLOW
        flow[0, x, rows, :] = jnp.where(is_pore, (W0 / RELAX_FLOW) * rho * base + keep * p[0], p[0])
        speeds = (ux, uy, uz, ux + uy, ux - uy, ux + uz, ux - uz, uy + uz, uy - uz)
        scaled1 = (W1 / RELAX_FLOW) * rho
        scaled2 = (W2 / RELAX_FLOW) * rho
        for n, (a, b) in enumerate(PAIRS):
            scaled = scaled1 if n < 3 else scaled2
            cu = speeds[n]
            even = scaled * (base + 4.5 * (cu * cu))
            odd = scaled * (3.0 * cu)
            flow[a, x, rows, :] = jnp.where(is_pore, (even + odd) + keep * p[a], p[a])
            flow[b, x, rows, :] = jnp.where(is_pore, (even - odd) + keep * p[b], p[b])
        h = [heat[d, x, rows, :] for d in range(7)]
        temp = h[0] + (h[1] + h[2]) + (h[3] + h[4]) + (h[5] + h[6])
        hkeep = 1.0 - 1.0 / RELAX_HEAT
        hot[0, x, rows, :] = jnp.where(is_pore, (0.25 / RELAX_HEAT) * temp + hkeep * h[0], h[0])
        even = (0.125 / RELAX_HEAT) * temp
        for n in range(3):
            a, b = PAIRS[n]
            odd = even * (4.0 * speeds[n])
            hot[a, x, rows, :] = jnp.where(is_pore, (even + odd) + hkeep * h[a], h[a])
            hot[b, x, rows, :] = jnp.where(is_pore, (even - odd) + hkeep * h[b], h[b])
        return carry

    lax.fori_loop(0, nx, plane, 0)


def edge_tile(low, high, row):
    return jnp.where(row < DEEP, low, high)


def pack_pairs(pairs, row):
    out = None
    for j, (low, high) in enumerate(pairs):
        if j:
            low, high = pltpu.roll(low, j, 0), pltpu.roll(high, TILE - j, 0)
        both = jnp.where(row < DEEP, low, high)
        out = both if out is None else jnp.where((row == j) | (row == TILE - 1 - j), both, out)
    return out


def heat_body(hot, flow, tsm, rows_in, new_heat, temp, bounce, zmsg, zflow):
    nx, nz, ny = tsm.shape
    rowz = rows8((nz, ny))
    row = rows8((TILE, ny))
    first, last = slice(0, TILE), slice(nz - TILE, nz)
    for x in range(nx):
        t = tsm[x]
        is_pore = t == 0.0
        g = [hot[d, x] for d in range(7)]
        own = WALL_OWN * (g[0] + (g[1] + g[2]) + (g[3] + g[4]) + (g[5] + g[6]))
        new_heat[0, x] = g[0]
        total = g[0]

        def arrive(d, near, moved):
            return jnp.where(near == 0.0, moved, (own - g[OPP[d]]) + WALL_NEAR * near)

        for d in (1, 2):
            src = x - DIRS[d][0]
            if 0 <= src < nx:
                got = arrive(d, tsm[src], hot[d, src])
                total = total + got
                new_heat[d, x] = jnp.where(is_pore, got, g[d])
            else:
                new_heat[d, x] = g[d]
                bounce[0 if x == 0 else 1] = own - g[OPP[d]]
        for d in (3, 4):
            by = DIRS[d][1] % ny
            got = arrive(d, pltpu.roll(t, by, 1), pltpu.roll(g[d], by, 1))
            total = total + got
            new_heat[d, x] = jnp.where(is_pore, got, g[d])
        for d in (5, 6):
            by = DIRS[d][2] % nz
            got = arrive(d, pltpu.roll(t, by, 0), pltpu.roll(g[d], by, 0))
            inside = rowz != (0 if d == 5 else nz - 1)
            total = total + jnp.where(inside, got, 0.0)
            new_heat[d, x] = jnp.where(is_pore & inside, got, g[d])
        total = jnp.where(is_pore, total, t)
        temp[x] = total
        zmsg[x] = edge_tile(total[first], total[last], row)
        pairs = [(g[6][first], g[5][last]), ((own - g[6])[first], (own - g[5])[last])]
        for up, down in ZPAIRS:
            pairs.append((flow[down, x, first, :], flow[up, x, last, :]))
        zmsg[nx + x] = pack_pairs(pairs[:4], row)
        zflow[x] = pack_pairs(pairs[4:], row)
    ends = (hot[2, 0], hot[1, nx - 1], bounce[0], bounce[1])
    for n, v in enumerate(ends):
        zmsg[2 * nx + n] = edge_tile(v[first], v[last], row)
    zmsg[2 * nx + 4 :] = rows_in[...]


def put_plane(out, n, v):
    tiles = v.shape[0] // TILE
    for i in range(tiles):
        out[n + i] = v[i * TILE : (i + 1) * TILE]
    return n + tiles


def get_plane(ref, n, tiles):
    return ref[n : n + tiles].reshape(tiles * TILE, ref.shape[-1])


def parity():
    return lax.axis_index("dev") % 2


def by_side(cross, intra, body):
    odd = parity()
    for value, (low, high) in enumerate(((cross, intra), (intra, cross))):

        @pl.when(odd == value)
        def _(low=low, high=high):
            body(low, high)


def picker(cross, intra):
    odd = parity()

    def pick(side, n, tiles):
        across, within = get_plane(cross, n, tiles), get_plane(intra, n, tiles)
        even_value, odd_value = (across, within) if side == 0 else (within, across)
        return jnp.where(jnp.full(across.shape, odd) == 0, even_value, odd_value)

    return pick


def early_body(km, flow, hot, bounce, temp, cross, intra):
    nx, nz = km.shape[:2]

    def fill(low, high):
        for side, out in ((0, low), (1, high)):
            n = 0
            deep = range(side * (nx - DEEP), side * (nx - DEEP) + DEEP)
            for x in deep:
                n = put_plane(out, n, km[x])
            for d in (XLOW, XHIGH)[side]:
                n = put_plane(out, n, flow[d, side * (nx - 1)])
            n = put_plane(out, n, hot[2 - side, side * (nx - 1)])
            n = put_plane(out, n, bounce[side])
            for x in deep:
                n = put_plane(out, n, temp[x, TILE : nz - TILE, :])

    by_side(cross, intra, fill)


def zjoin_body(mine, theirs, temp, heat_in, after, heat_ends, joined, cross, intra):
    nx, nz, ny = temp.shape
    row = rows8((TILE, ny))
    edge = (row == 0) | (row == TILE - 1)
    first, last = slice(0, TILE), slice(nz - TILE, nz)

    def swap(v):
        return jnp.where(row < DEEP, pltpu.roll(v, 1, 0), pltpu.roll(v, TILE - 1, 0))

    def slot1(v):
        return jnp.where(row < DEEP, pltpu.roll(v, TILE - 1, 0), pltpu.roll(v, 1, 0))

    for x in range(nx):
        my_k, their_k = mine[2 * nx + 4 + x], theirs[2 * nx + 4 + x]
        my_t, their_t = jnp.where(my_k == 0.0, 0.0, mine[x]), jnp.where(their_k == 0.0, 0.0, theirs[x])
        my_p, their_p = mine[nx + x], theirs[nx + x]
        near = swap(their_t)
        got = jnp.where(near == 0.0, swap(their_p), slot1(my_p) + WALL_NEAR * near)
        mine_in = edge & (my_t == 0.0)
        add = jnp.where(mine_in, got, 0.0)
        near = swap(my_t)
        back = jnp.where(near == 0.0, swap(my_p), slot1(their_p) + WALL_NEAR * near)
        back = jnp.where(edge & (their_t == 0.0), back, 0.0)
        heat_ends[0, x] = jnp.where(mine_in & (row == 0), got, heat_in[5, x, first, :])
        heat_ends[1, x] = jnp.where(mine_in & (row == TILE - 1), got, heat_in[6, x, last, :])
        joined[x, first, :] = temp[x, first, :] + jnp.where(row == 0, add, 0.0)
        joined[x, TILE : nz - TILE, :] = temp[x, TILE : nz - TILE, :]
        joined[x, last, :] = temp[x, last, :] + jnp.where(row == TILE - 1, add, 0.0)
        joined[x, nz : nz + TILE, :] = theirs[x] + back

    def fill(low, high):
        for side, out in ((0, low), (1, high)):
            for n in range(DEEP):
                v = joined.at[side * (nx - DEEP) + n]
                out[3 * n] = v[first, :]
                out[3 * n + 1] = v[last, :]
                out[3 * n + 2] = v[nz : nz + TILE, :]
            n = 3 * DEEP
            out[n] = theirs[2 * nx + side]
            out[n + 1] = theirs[2 * nx + 2 + side]
            v = theirs[nx + side * (nx - 1)]
            lower, upper = (5, 2) if side else (6, 3)
            out[n + 2] = jnp.where(row < DEEP, pltpu.roll(v, lower, 0), pltpu.roll(v, upper, 0))
            base = 2 * nx + 4 + side * (nx - DEEP)
            out[n + 3 : n + 3 + DEEP] = theirs[base : base + DEEP]

    by_side(cross, intra, fill)


def reader(nx, early, late, tsm, km, rows):
    tiles = km.shape[1] // TILE
    ahead = (DEEP + len(XLOW)) * tiles
    corner = 3 * DEEP + 3

    def away(p):
        return (0, p) if p < DEEP else (1, p - DEEP - nx)

    def km_halo(p):
        if DEEP <= p < DEEP + nx:
            return rows[2 * nx + 4 + p - DEEP]
        side, n = away(p)
        return late(side, corner + n, 1)

    def km_at(p):
        if DEEP <= p < DEEP + nx:
            core = km[p - DEEP]
        else:
            side, n = away(p)
            core = early(side, n * tiles, tiles)
        return jnp.concatenate([core, km_halo(p)], axis=0)

    def temp_far(p):
        side, n = away(p)
        middle = early(side, ahead + 2 * tiles + n * (tiles - 2), tiles - 2)
        ends = late(side, 3 * n, 3)
        return jnp.concatenate([ends[0:TILE], middle, ends[TILE:]], axis=0)

    def ts_at(p):
        if DEEP <= p < DEEP + nx:
            halo = jnp.where(km_halo(p) == 0.0, 0.0, rows[p - DEEP])
            return jnp.concatenate([tsm[p - DEEP], halo], axis=0)
        return jnp.where(km_at(p) == 0.0, 0.0, temp_far(p))

    return ts_at, km_at, km_halo, temp_far, ahead


def face(a, b):
    return (2.0 * a) * b / jnp.maximum(a + b, 1.0)


def still_plane(ts_at, km_at, p, fx_low, fx_high):
    k, t = km_at(p), ts_at(p)
    ext, ny = k.shape
    k_low, k_high = pltpu.roll(k, 1, 1), pltpu.roll(k, ny - 1, 1)
    count = jnp.where(k_low == 0.0, 1.0, 0.0) + jnp.where(k_high == 0.0, 1.0, 0.0)
    y_low, y_high = face(k, k_low), face(k, k_high)
    k_low, k_high = pltpu.roll(k, 1, 0), pltpu.roll(k, ext - 1, 0)
    count = count + (jnp.where(k_low == 0.0, 1.0, 0.0) + jnp.where(k_high == 0.0, 1.0, 0.0))
    z_low = face(k, k_low)
    z_high = pltpu.roll(z_low, ext - 1, 0)
    count = count + (jnp.where(km_at(p - 1) == 0.0, 1.0, 0.0) + jnp.where(km_at(p + 1) == 0.0, 1.0, 0.0))
    total = (fx_low + fx_high) + (y_low + y_high) + (z_low + z_high)
    near = spread(t, ts_at(p - 1), ts_at(p + 1), fx_low, fx_high, y_low, y_high, z_low, z_high)
    return y_low, y_high, z_low, z_high, 1.0 + total, near - (FILM * count + total) * t


def spread(v, below, above, fx_low, fx_high, y_low, y_high, z_low, z_high):
    ext, ny = v.shape
    in_y = y_low * pltpu.roll(v, 1, 1) + y_high * pltpu.roll(v, ny - 1, 1)
    in_z = z_low * pltpu.roll(v, 1, 0) + z_high * pltpu.roll(v, ext - 1, 0)
    return (fx_low * below + fx_high * above) + in_z + in_y


def static_body(tsm, km, theirs, fx, *outs):
    nx = tsm.shape[0]
    ts_at, km_at = reader(nx, None, None, tsm, km, theirs)[:2]
    first = DEEP + 1
    for n in range(nx - 1):
        fx[n] = face(km_at(first + n), km_at(first + n - 1))
    for n in range(nx - 2):
        for out, v in zip(outs, still_plane(ts_at, km_at, first + n, fx[n], fx[n + 1])):
            out[n] = v


def conduct_body(*all_refs):
    early_cross, early_intra, late_cross, late_intra, theirs, joined, bounce = all_refs[0:7]
    in_fx, in_still = all_refs[7], all_refs[8:14]
    tsm, km, hot, ts, corners, heat_in, pops_in, new_heat, new_pops, new_solid = all_refs[14:24]
    temp, resid, step_a, step_b, fx = all_refs[24:29]
    still, (total, ends, patched, sems) = all_refs[29:35], all_refs[35:]
    nx, nz, ny = ts.shape
    planes, ext = temp.shape[:2]
    tiles = nz // TILE
    own = slice(0, nz)
    early, late = picker(early_cross, early_intra), picker(late_cross, late_intra)
    ts_at, km_at, km_halo, temp_far, ahead = reader(nx, early, late, tsm, km, theirs)

    def ready(p):
        return DEEP < p < DEEP + nx - 1

    def fx_at(p):
        return in_fx[p - DEEP - 1] if DEEP < p < DEEP + nx else fx[p]

    def still_at(n, p):
        return in_still[n][p - DEEP - 1] if ready(p) else still[n][p]

    def apply(v, p, now):
        near = spread(v, now[p - 1], now[p + 1], fx_at(p), fx_at(p + 1), *(still_at(n, p) for n in range(4)))
        return near - still_at(4, p) * v

    def temp_at(p):
        return joined[p - DEEP] if DEEP <= p < DEEP + nx else temp_far(p)

    def sent(n, side):
        return jnp.concatenate([early(side, ahead + n * tiles, tiles), late(side, 3 * DEEP + n, 1)], axis=0)

    def mine(n, side):
        end = (hot[2 - side, side * (nx - 1)], bounce[side])[n]
        return jnp.concatenate([end, theirs[2 * nx + 2 * n + side]], axis=0)

    def join(side):
        p_own = DEEP + side * (nx - 1)
        p_far = p_own - 1 + 2 * side
        t_own, t_far = ts_at(p_own), ts_at(p_far)
        got = jnp.where(t_far == 0.0, sent(0, side), mine(1, side) + WALL_NEAR * t_far)
        back = jnp.where(t_own == 0.0, mine(0, side), sent(1, side) + WALL_NEAR * t_own)
        temp[p_own] = jnp.where(t_own == 0.0, temp_at(p_own) + got, 0.0)
        temp[p_far] = jnp.where(t_far == 0.0, temp_at(p_far) + back, 0.0)
        return got

    row = rows8((TILE, ny))
    corner = 3 * DEEP + 2
    copies = []
    for n, (d, x, p, side) in enumerate(
        (
            (11, 0, DEEP - 1, 0),
            (13, 0, DEEP - 1, 0),
            (12, nx - 1, DEEP + nx, 1),
            (14, nx - 1, DEEP + nx, 1),
        )
    ):
        by, at, rows = (1, 0, slice(0, TILE)) if DIRS[d][2] > 0 else (TILE - 1, TILE - 1, slice(nz - TILE, nz))
        there = pltpu.roll(km_halo(p), by, 0)
        both = (row == at) & (tsm[x, rows, :] == 0.0) & (there == 0.0)
        patched[n] = jnp.where(both, pltpu.roll(late(side, corner, 1), by, 0), corners[n])
        copies.append(pltpu.make_async_copy(patched.at[n], new_pops.at[d, x, rows, :], sems.at[n]))
        copies[-1].start()
    for p in range(planes):
        if p not in (DEEP - 1, DEEP, DEEP + nx - 1, DEEP + nx):
            temp[p] = jnp.where(km_at(p) == 0.0, temp_at(p), 0.0)
    up, down = join(0), join(1)
    ends[0] = jnp.where(tsm[0] == 0.0, up[own], hot[1, 0])
    ends[1] = jnp.where(tsm[nx - 1] == 0.0, down[own], hot[2, nx - 1])
    for n, (d, x) in enumerate(((1, 0), (2, nx - 1))):
        copies.append(pltpu.make_async_copy(ends.at[n], new_heat.at[d, x], sems.at[4 + n]))
        copies[-1].start()

    for p in range(1, planes):
        if not DEEP < p < DEEP + nx:
            fx[p] = face(km_at(p), km_at(p - 1))
    for p in range(1, planes - 1):
        if not ready(p):
            for out, v in zip(still, still_plane(ts_at, km_at, p, fx_at(p), fx_at(p + 1))):
                out[p] = v

    def residual(p):
        mid = temp[p]
        near = (temp[p - 1] + temp[p + 1]) + (pltpu.roll(mid, 1, 0) + pltpu.roll(mid, ext - 1, 0))
        near = near + (pltpu.roll(mid, 1, 1) + pltpu.roll(mid, ny - 1, 1))
        return jnp.where(km_at(p) == 0.0, 0.0, FILM * near) + still_at(5, p)

    def pairs(start):
        every = list(range(start, planes - start))
        return [every[n : n + 2] for n in range(0, len(every), 2)]

    for group in pairs(1):
        for p, r in [(p, residual(p)) for p in group]:
            resid[p] = r
            s = r * (1.0 / THETA)
            step_a[p] = s
            if DEEP <= p < DEEP + nx:
                total[p - DEEP] = ts[p - DEEP] + s[own]
    sigma = THETA / DELTA
    ratio = 1.0 / sigma
    now, later = step_a, step_b
    for sweep in range(1, ITERS):
        after = 1.0 / (2.0 * sigma - ratio)
        for group in pairs(1 + sweep):
            done = []
            for p in group:
                v = now[p]
                r = resid[p] + apply(v, p, now)
                done.append((p, r, (after * ratio) * v + (2.0 * after / DELTA) * r))
            for p, r, s in done:
                if sweep + 1 < ITERS:
                    resid[p] = r
                    later[p] = s
                if DEEP <= p < DEEP + nx:
                    x = p - DEEP
                    total[x] = total[x] + s[own]
                    if sweep + 1 == ITERS:
                        copies.append(pltpu.make_async_copy(total.at[x], new_solid.at[x], sems.at[6 + x]))
                        copies[-1].start()
        ratio = after
        now, later = later, now
    for copy in copies:
        copy.wait()


FLOW_DIRS = (
    (0, 1, 2, 3, 4, 7, 8, 9, 10),
    (5, 6, 11, 12, 13, 14, 15, 16, 17, 18),
    tuple(range(19)),
)
FLOW_RUNS = (((0, 5), (7, 4)), ((5, 2), (11, 8)), ((0, 19),))


def flow_body(part, *all_refs):
    early = theirs = None
    if part == 0:
        flow, tsm, out, turned, buf, sems = all_refs
    elif part == 1:
        flow, tsm, theirs, flow_rows, turned, heat, heat_ends, held, out, heat_out, buf, sems, heat_sems = all_refs
    else:
        flow, tsm, theirs, flow_rows, turned, early_cross, early_intra, held, out, corners, buf, sems = all_refs
        early = picker(early_cross, early_intra)
    nx, nz, ny = flow.shape[1:]
    tiles = nz // TILE
    row = rows8((TILE, ny))
    if part == 0:
        for x in range(nx):
            for n, by in enumerate((1, ny - 1)):
                turned[n, x] = pltpu.roll(tsm[x], by, 1)
    if part == 1:
        copy_heat = pltpu.make_async_copy(heat, heat_out, heat_sems.at[0])
        copy_heat.start()

    def span(i):
        return slice(i * TILE, (i + 1) * TILE)

    def turn(v, cy):
        return pltpu.roll(v, cy % ny, 1) if cy else v

    def shift(tile, i, cz):
        if not cz:
            return tile(i)
        far, by = (0, 1) if cz > 0 else (TILE - 1, TILE - 1)
        return jnp.where(row == far, pltpu.roll(tile(i - cz), by, 0), pltpu.roll(tile(i), by, 0))

    def mask_tile(q, cy, i):
        if not 0 <= q < nx:
            return turn(early(int(q > 0), (0 if q > 0 else DEEP - 1) * tiles + i % tiles, 1), cy)
        if not 0 <= i < tiles:
            return turn(theirs[2 * nx + 4 + q], cy)
        if cy:
            return turned[0 if cy > 0 else 1, q, span(i), :]
        return tsm[q, span(i), :]

    def flow_tile(d, q, i):
        if 0 <= q < nx:
            if 0 <= i < tiles:
                return flow[d, q, span(i), :]
            v = theirs[nx + q] if d in (11, 12, 13, 14) else flow_rows[q]
            by = ZSLOT[d] if DIRS[d][2] > 0 else TILE - ZSLOT[d]
            return pltpu.roll(v, by % TILE, 0) if by % TILE else v
        side, n = (0, XHIGH.index(d)) if q < 0 else (1, XLOW.index(d))
        return early(side, (DEEP + n) * tiles + i % tiles, 1)

    copies = []
    for at, x in enumerate(range(1, nx - 1) if part < 2 else (0, nx - 1)):
        slot = at
        for i in range(tiles):
            is_pore = tsm[x, span(i), :] == 0.0
            done = []
            for at_d, d in enumerate(FLOW_DIRS[part]):
                if d == 0:
                    done.append(flow[0, x, span(i), :])
                    continue
                cx, cy, cz = DIRS[d]
                q = x - cx
                t = shift(lambda n: mask_tile(q, cy, n), i, cz)
                both = is_pore & (t == 0.0)
                v = turn(shift(lambda n: flow_tile(d, q, n), i, cz), cy)
                open_row = cz and not 0 <= q < nx and i == (0 if cz > 0 else tiles - 1)
                if open_row:
                    both = both & (row != (0 if cz > 0 else TILE - 1))
                v = jnp.where(both, v, jnp.where(is_pore, flow[OPP[d], x, span(i), :], flow[d, x, span(i), :]))
                done.append(v)
                if open_row:
                    corners[(11, 13, 12, 14).index(d)] = v
            for at_d, v in enumerate(done):
                buf[slot, at_d, span(i), :] = v
        begin = 0
        copies.append([])
        for n, (d, count) in enumerate(FLOW_RUNS[part]):
            src, dst = buf.at[slot, begin : begin + count], out.at[d : d + count, x]
            copies[-1].append(pltpu.make_async_copy(src, dst, sems.at[2 * slot + n]))
            copies[-1][-1].start()
            begin += count
    if part == 1:
        copy_heat.wait()
        for n, rows in ((0, slice(0, TILE)), (1, slice(nz - TILE, nz))):
            copy = pltpu.make_async_copy(heat_ends.at[n], heat_out.at[5 + n, :, rows, :], heat_sems.at[n])
            copy.start()
            copies[-1].append(copy)
    for group in copies:
        for copy in group:
            copy.wait()


def ring(axis, by):
    count = lax.axis_size(axis)
    return [(i, (i + by) % count) for i in range(count)]


def along_z(rows):
    if lax.axis_size("grp") == 2:
        return lax.ppermute(rows, "grp", ring("grp", 1))
    from_below = lax.ppermute(rows, "grp", ring("grp", 1))
    from_above = lax.ppermute(rows, "grp", ring("grp", -1))
    upper = lax.broadcasted_iota(jnp.int32, rows.shape, 1) < DEEP
    return jnp.where(upper, from_above, from_below)


def along_x(cross, intra):
    count = lax.axis_size("dev")
    across = [(i, (i + 2 * (i % 2) - 1) % count) for i in range(count)]
    return lax.ppermute(cross, "dev", across), lax.ppermute(intra, "dev", [(i, i ^ 1) for i in range(count)])


def per_device(populations, heat_pops, solid_temp, conductivity, pore_mask):
    nx, nz, ny = solid_temp.shape
    ext = nz + TILE
    tiles = ext // TILE
    planes = nx + 2 * DEEP
    field = (nx, nz, ny)
    wide = (planes, ext, ny)
    dma = pltpu.SemaphoreType.DMA
    flow, hot, tsm, km, my_rows = call(
        collide_body,
        [(19, *field), (7, *field), field, field, (nx, TILE, ny)],
        [pltpu.with_memory_space_constraint(v, pltpu.HBM) for v in (populations, heat_pops, solid_temp, conductivity, pore_mask)],
        in_specs=[HBM] * 5,
        scratch=[
            pltpu.VMEM((19, *field), jnp.float32),
            pltpu.VMEM((7, *field), jnp.float32),
            pltpu.VMEM(field, jnp.float32),
            pltpu.VMEM(field, jnp.float32),
            pltpu.VMEM(field, jnp.int32),
            dma((3 + 2 * nx,)),
        ],
        limit=12 << 20,
        us=4,
    )
    new_heat, temp, bounce, zmsg, zflow = call(
        heat_body,
        [(7, *field), field, (2, nz, ny), (3 * nx + 4, TILE, ny), (nx, TILE, ny)],
        [hot, flow, tsm, my_rows],
    )
    theirs = along_z(zmsg)
    flow_rows = along_z(zflow)
    early_shape = ((DEEP + len(XLOW) + 2) * (tiles - 1) + DEEP * (tiles - 3), TILE, ny)
    early = along_x(*call(early_body, [early_shape] * 2, [km, flow, hot, bounce, temp]))

    def flow_call(part, outs, args, out_specs, in_hbm=0, extra=(), **rest):
        held = (2 if part == 2 else nx - 2, len(FLOW_DIRS[part]), nz, ny)
        return call(
            functools.partial(flow_body, part),
            outs,
            args,
            in_specs=[VM] * (len(args) - in_hbm) + [ANY] * in_hbm,
            out_specs=out_specs,
            scratch=[pltpu.VMEM(held, jnp.float32), dma((2 * nx,)), *extra],
            limit=6 << 20,
            **rest,
        )

    pops_shape, heat_shape = (19, *field), (7, *field)
    new_pops, turned = flow_call(0, [pops_shape, (2, *field)], [flow, tsm], [ANY, VM], us=20)
    late_shape = (4 * DEEP + 3, TILE, ny)
    heat_ends, joined, cross, intra = call(
        zjoin_body,
        [(2, nx, TILE, ny), (nx, ext, ny), late_shape, late_shape],
        [zmsg, theirs, temp, new_heat, turned],
        us=50,
    )
    late = along_x(cross, intra)
    new_pops, new_heat = flow_call(
        1,
        [pops_shape, heat_shape],
        [flow, tsm, theirs, flow_rows, turned, new_heat, heat_ends, new_pops],
        [ANY, ANY],
        in_hbm=1,
        extra=[dma((2,))],
        aliases={7: 0},
        us=20,
    )
    new_pops, corners = flow_call(
        2,
        [pops_shape, (4, TILE, ny)],
        [flow, tsm, theirs, flow_rows, turned, *early, new_pops],
        [ANY, VM],
        in_hbm=1,
        aliases={7: 0},
    )
    fixed = call(
        static_body,
        [(nx - 1, ext, ny)] + [(nx - 2, ext, ny)] * 6,
        [tsm, km, theirs],
    )
    new_heat, new_pops, new_solid = call(
        conduct_body,
        [heat_shape, pops_shape, field],
        [*early, *late, theirs, joined, bounce, *fixed, tsm, km, hot, solid_temp, corners, new_heat, new_pops],
        in_specs=[VM] * 19 + [ANY] * 2,
        out_specs=[ANY, ANY, ANY],
        scratch=[pltpu.VMEM(wide, jnp.float32)] * 11
        + [pltpu.VMEM(field, jnp.float32), pltpu.VMEM((2, nz, ny), jnp.float32), pltpu.VMEM((4, TILE, ny), jnp.float32)]
        + [dma((6 + nx,))],
        aliases={19: 0, 20: 1},
        limit=12 << 20,
        us=4,
    )
    return new_pops, new_heat, new_solid


def solution(mesh):
    wide = P(None, "dev", "grp", None)
    flat = P("dev", "grp", None)
    return jax.shard_map(
        per_device,
        mesh=mesh,
        in_specs=(wide, wide, flat, flat, flat),
        out_specs=(wide, wide, flat),
        check_vma=False,
    )
```

```python
import functools

import jax
import jax.numpy as jnp
from jax import lax
from jax.experimental import pallas as pl
from jax.experimental.pallas import tpu as pltpu
from jax.sharding import PartitionSpec as P

ITERS = 4
DIRS = (
    (0, 0, 0),
    (1, 0, 0),
    (-1, 0, 0),
    (0, 1, 0),
    (0, -1, 0),
    (0, 0, 1),
    (0, 0, -1),
    (1, 1, 0),
    (-1, -1, 0),
    (1, -1, 0),
    (-1, 1, 0),
    (1, 0, 1),
    (-1, 0, -1),
    (1, 0, -1),
    (-1, 0, 1),
    (0, 1, 1),
    (0, -1, -1),
    (0, 1, -1),
    (0, -1, 1),
)
OPP = (0, 2, 1, 4, 3, 6, 5, 8, 7, 10, 9, 12, 11, 14, 13, 16, 15, 18, 17)
PAIRS = ((1, 2), (3, 4), (5, 6), (7, 8), (9, 10), (11, 12), (13, 14), (15, 16), (17, 18))
ZPAIRS = ((11, 12), (14, 13), (5, 6), (15, 16), (18, 17))
ZSLOT = {11: 2, 12: 2, 14: 3, 13: 3, 5: 0, 6: 0, 15: 1, 16: 1, 18: 2, 17: 2}
XHIGH = (1, 7, 9, 11, 13)
XLOW = (2, 8, 10, 12, 14)
W0, W1, W2 = 1.0 / 3.0, 1.0 / 18.0, 1.0 / 36.0
RELAX_FLOW = 0.8
RELAX_HEAT = 0.7
JUMP = 0.3
FILM = 0.5
THETA = 61.0
DELTA = 60.0
WALL_OWN = 0.25 * JUMP
WALL_NEAR = 0.25 * (1.0 - JUMP)
DEEP = 4
HALO = DEEP - 1
TILE = 8

VM = pl.BlockSpec(memory_space=pltpu.VMEM)
ANY = pl.BlockSpec(memory_space=pl.ANY)
HBM = pl.BlockSpec(memory_space=pltpu.HBM)


def call(body, outs, args, in_specs=None, out_specs=None, scratch=(), aliases=None, limit=4 << 20, us=0.5):
    return pl.pallas_call(
        body,
        out_shape=[jax.ShapeDtypeStruct(shape, jnp.float32) for shape in outs],
        in_specs=in_specs or [VM] * len(args),
        out_specs=out_specs or [VM] * len(outs),
        scratch_shapes=list(scratch),
        input_output_aliases=aliases or {},
        compiler_params=pltpu.CompilerParams(vmem_limit_bytes=limit),
        cost_estimate=pl.CostEstimate(flops=int(us * 1e9), bytes_accessed=int(us * 3e6), transcendentals=0),
    )(*args)


def rows8(shape):
    return lax.broadcasted_iota(jnp.int32, shape, 0)


def collide_body(*refs):
    sources, (flow, hot, tsm, km, rows_out), held, sems = refs[:5], refs[5:10], refs[10:15], refs[15]
    pops, heat, ts, cond, pore = held
    nx, nz, ny = tsm.shape
    row = rows8((TILE, ny))

    def fetch(n, x):
        if n < 2:
            return pltpu.make_async_copy(sources[n].at[:, x], held[n].at[:, x], sems.at[3 + n * nx + x])
        return pltpu.make_async_copy(sources[n], held[n], sems.at[n - 2])

    for n in (2, 3, 4):
        fetch(n, 0).start()
    for x in range(nx):
        for n in (0, 1):
            fetch(n, x).start()
    for n in (2, 3, 4):
        fetch(n, 0).wait()

    def plane(x, carry):
        is_pore = pore[x] != 0
        for n, (src, dst) in enumerate(((ts, tsm), (cond, km))):
            v = jnp.where(is_pore, 0.0, src[x])
            dst[x] = v
            if n:
                rows_out[x] = edge_tile(v[0:TILE], v[nz - TILE : nz], row)
        for n in (0, 1):
            fetch(n, x).wait()
        return lax.fori_loop(0, nz // TILE, lambda i, c: step(x, i, c), carry)

    def step(x, i, carry):
        rows = pl.ds(pl.multiple_of(i * TILE, TILE), TILE)
        is_pore = tsm[x, rows, :] == 0.0
        p = [pops[d, x, rows, :] for d in range(19)]
        diff = [p[a] - p[b] for a, b in PAIRS]
        rho = p[0]
        for a, b in PAIRS:
            rho = rho + (p[a] + p[b])
        inv = 1.0 / rho
        ux = (diff[0] + diff[3] + diff[4] + diff[5] + diff[6]) * inv
        uy = (diff[1] + diff[3] - diff[4] + diff[7] + diff[8]) * inv
        uz = (diff[2] + diff[5] - diff[6] + diff[7] - diff[8]) * inv
        base = 1.0 - 1.5 * (ux * ux + uy * uy + uz * uz)
        keep = 1.0 - 1.0 / RELAX_FLOW
        flow[0, x, rows, :] = jnp.where(is_pore, (W0 / RELAX_FLOW) * rho * base + keep * p[0], p[0])
        speeds = (ux, uy, uz, ux + uy, ux - uy, ux + uz, ux - uz, uy + uz, uy - uz)
        scaled1 = (W1 / RELAX_FLOW) * rho
        scaled2 = (W2 / RELAX_FLOW) * rho
        for n, (a, b) in enumerate(PAIRS):
            scaled = scaled1 if n < 3 else scaled2
            cu = speeds[n]
            even = scaled * (base + 4.5 * (cu * cu))
            odd = scaled * (3.0 * cu)
            flow[a, x, rows, :] = jnp.where(is_pore, (even + odd) + keep * p[a], p[a])
            flow[b, x, rows, :] = jnp.where(is_pore, (even - odd) + keep * p[b], p[b])
        h = [heat[d, x, rows, :] for d in range(7)]
        temp = h[0] + (h[1] + h[2]) + (h[3] + h[4]) + (h[5] + h[6])
        hkeep = 1.0 - 1.0 / RELAX_HEAT
        hot[0, x, rows, :] = jnp.where(is_pore, (0.25 / RELAX_HEAT) * temp + hkeep * h[0], h[0])
        even = (0.125 / RELAX_HEAT) * temp
        for n in range(3):
            a, b = PAIRS[n]
            odd = even * (4.0 * speeds[n])
            hot[a, x, rows, :] = jnp.where(is_pore, (even + odd) + hkeep * h[a], h[a])
            hot[b, x, rows, :] = jnp.where(is_pore, (even - odd) + hkeep * h[b], h[b])
        return carry

    lax.fori_loop(0, nx, plane, 0)


def edge_tile(low, high, row):
    return jnp.where(row < DEEP, low, high)


def pack_pairs(pairs, row):
    out = None
    for j, (low, high) in enumerate(pairs):
        if j:
            low, high = pltpu.roll(low, j, 0), pltpu.roll(high, TILE - j, 0)
        both = jnp.where(row < DEEP, low, high)
        out = both if out is None else jnp.where((row == j) | (row == TILE - 1 - j), both, out)
    return out


def heat_body(hot, flow, tsm, rows_in, new_heat, temp, bounce, zmsg, zflow):
    nx, nz, ny = tsm.shape
    rowz = rows8((nz, ny))
    row = rows8((TILE, ny))
    first, last = slice(0, TILE), slice(nz - TILE, nz)
    for x in range(nx):
        t = tsm[x]
        is_pore = t == 0.0
        g = [hot[d, x] for d in range(7)]
        own = WALL_OWN * (g[0] + (g[1] + g[2]) + (g[3] + g[4]) + (g[5] + g[6]))
        new_heat[0, x] = g[0]
        total = g[0]

        def arrive(d, near, moved):
            return jnp.where(near == 0.0, moved, (own - g[OPP[d]]) + WALL_NEAR * near)

        for d in (1, 2):
            src = x - DIRS[d][0]
            if 0 <= src < nx:
                got = arrive(d, tsm[src], hot[d, src])
                total = total + got
                new_heat[d, x] = jnp.where(is_pore, got, g[d])
            else:
                new_heat[d, x] = g[d]
                bounce[0 if x == 0 else 1] = own - g[OPP[d]]
        for d in (3, 4):
            by = DIRS[d][1] % ny
            got = arrive(d, pltpu.roll(t, by, 1), pltpu.roll(g[d], by, 1))
            total = total + got
            new_heat[d, x] = jnp.where(is_pore, got, g[d])
        for d in (5, 6):
            by = DIRS[d][2] % nz
            got = arrive(d, pltpu.roll(t, by, 0), pltpu.roll(g[d], by, 0))
            inside = rowz != (0 if d == 5 else nz - 1)
            total = total + jnp.where(inside, got, 0.0)
            new_heat[d, x] = jnp.where(is_pore & inside, got, g[d])
        total = jnp.where(is_pore, total, t)
        temp[x] = total
        zmsg[x] = edge_tile(total[first], total[last], row)
        pairs = [(g[6][first], g[5][last]), ((own - g[6])[first], (own - g[5])[last])]
        for up, down in ZPAIRS:
            pairs.append((flow[down, x, first, :], flow[up, x, last, :]))
        zmsg[nx + x] = pack_pairs(pairs[:4], row)
        zflow[x] = pack_pairs(pairs[4:], row)
    ends = (hot[2, 0], hot[1, nx - 1], bounce[0], bounce[1])
    for n, v in enumerate(ends):
        zmsg[2 * nx + n] = edge_tile(v[first], v[last], row)
    zmsg[2 * nx + 4 :] = rows_in[...]


def put_plane(out, n, v):
    tiles = v.shape[0] // TILE
    for i in range(tiles):
        out[n + i] = v[i * TILE : (i + 1) * TILE]
    return n + tiles


def get_plane(ref, n, tiles):
    return ref[n : n + tiles].reshape(tiles * TILE, ref.shape[-1])


def parity():
    return lax.axis_index("dev") % 2


def by_side(cross, intra, body):
    odd = parity()
    for value, (low, high) in enumerate(((cross, intra), (intra, cross))):

        @pl.when(odd == value)
        def _(low=low, high=high):
            body(low, high)


def picker(cross, intra):
    odd = parity()

    def pick(side, n, tiles):
        across, within = get_plane(cross, n, tiles), get_plane(intra, n, tiles)
        even_value, odd_value = (across, within) if side == 0 else (within, across)
        return jnp.where(jnp.full(across.shape, odd) == 0, even_value, odd_value)

    return pick


def face(a, b):
    return (2.0 * a) * b / jnp.maximum(a + b, 1.0)


def beyond(k, k_far, temp, temp_far):
    rate = jnp.where(k_far == 0.0, FILM, face(k, k_far))
    return jnp.where(k == 0.0, 0.0, rate * (temp_far - temp))


def early_body(km, flow, hot, bounce, temp, cross, intra):
    nx, nz = km.shape[:2]

    def fill(low, high):
        for side, out in ((0, low), (1, high)):
            n = 0
            deep = range(side * (nx - HALO), side * (nx - HALO) + HALO)
            for x in deep:
                n = put_plane(out, n, km[x])
            for d in (XLOW, XHIGH)[side]:
                n = put_plane(out, n, flow[d, side * (nx - 1)])
            n = put_plane(out, n, hot[2 - side, side * (nx - 1)])
            n = put_plane(out, n, bounce[side])
            middle = slice(TILE, nz - TILE)
            for x in deep:
                n = put_plane(out, n, temp[x, middle, :])
            x, far = (HALO - 1, HALO) if side == 0 else (nx - HALO, nx - DEEP)
            put_plane(out, n, beyond(km[x, middle, :], km[far, middle, :], temp[x, middle, :], temp[far, middle, :]))

    by_side(cross, intra, fill)


def zjoin_body(mine, theirs, temp, km, heat_in, after, heat_ends, joined, cross, intra):
    nx, nz, ny = temp.shape
    row = rows8((TILE, ny))
    edge = (row == 0) | (row == TILE - 1)
    first, last = slice(0, TILE), slice(nz - TILE, nz)

    def swap(v):
        return jnp.where(row < DEEP, pltpu.roll(v, 1, 0), pltpu.roll(v, TILE - 1, 0))

    def slot1(v):
        return jnp.where(row < DEEP, pltpu.roll(v, TILE - 1, 0), pltpu.roll(v, 1, 0))

    for x in range(nx):
        my_k, their_k = mine[2 * nx + 4 + x], theirs[2 * nx + 4 + x]
        my_t, their_t = jnp.where(my_k == 0.0, 0.0, mine[x]), jnp.where(their_k == 0.0, 0.0, theirs[x])
        my_p, their_p = mine[nx + x], theirs[nx + x]
        near = swap(their_t)
        got = jnp.where(near == 0.0, swap(their_p), slot1(my_p) + WALL_NEAR * near)
        mine_in = edge & (my_t == 0.0)
        add = jnp.where(mine_in, got, 0.0)
        near = swap(my_t)
        back = jnp.where(near == 0.0, swap(my_p), slot1(their_p) + WALL_NEAR * near)
        back = jnp.where(edge & (their_t == 0.0), back, 0.0)
        heat_ends[0, x] = jnp.where(mine_in & (row == 0), got, heat_in[5, x, first, :])
        heat_ends[1, x] = jnp.where(mine_in & (row == TILE - 1), got, heat_in[6, x, last, :])
        joined[x, first, :] = temp[x, first, :] + jnp.where(row == 0, add, 0.0)
        joined[x, TILE : nz - TILE, :] = temp[x, TILE : nz - TILE, :]
        joined[x, last, :] = temp[x, last, :] + jnp.where(row == TILE - 1, add, 0.0)
        joined[x, nz : nz + TILE, :] = theirs[x] + back

    def fill(low, high):
        for side, out in ((0, low), (1, high)):
            for n in range(HALO):
                v = joined.at[side * (nx - HALO) + n]
                out[3 * n] = v[first, :]
                out[3 * n + 1] = v[last, :]
                out[3 * n + 2] = v[nz : nz + TILE, :]
            x, far = (HALO - 1, HALO) if side == 0 else (nx - HALO, nx - DEEP)
            n = 3 * HALO
            for rows in (first, last):
                out[n] = beyond(km[x, rows, :], km[far, rows, :], joined[x, rows, :], joined[far, rows, :])
                n += 1
            out[n] = theirs[2 * nx + side]
            out[n + 1] = theirs[2 * nx + 2 + side]
            v = theirs[nx + side * (nx - 1)]
            lower, upper = (5, 2) if side else (6, 3)
            out[n + 2] = jnp.where(row < DEEP, pltpu.roll(v, lower, 0), pltpu.roll(v, upper, 0))
            base = 2 * nx + 4 + side * (nx - HALO)
            out[n + 3 : n + 3 + HALO] = theirs[base : base + HALO]

    by_side(cross, intra, fill)


def reader(nx, early, late, tsm, km, rows):
    tiles = km.shape[1] // TILE
    ahead = (HALO + len(XLOW)) * tiles
    corner = 3 * HALO + 5

    def away(p):
        return (0, p - 1) if p < DEEP else (1, p - DEEP - nx)

    def km_halo(p):
        if DEEP <= p < DEEP + nx:
            return rows[2 * nx + 4 + p - DEEP]
        side, n = away(p)
        return late(side, corner + n, 1)

    def km_at(p):
        if DEEP <= p < DEEP + nx:
            core = km[p - DEEP]
        else:
            side, n = away(p)
            core = early(side, n * tiles, tiles)
        return jnp.concatenate([core, km_halo(p)], axis=0)

    def temp_far(p):
        side, n = away(p)
        middle = early(side, ahead + 2 * tiles + n * (tiles - 2), tiles - 2)
        ends = late(side, 3 * n, 3)
        return jnp.concatenate([ends[0:TILE], middle, ends[TILE:]], axis=0)

    def ts_at(p):
        if DEEP <= p < DEEP + nx:
            halo = jnp.where(km_halo(p) == 0.0, 0.0, rows[p - DEEP])
            return jnp.concatenate([tsm[p - DEEP], halo], axis=0)
        return jnp.where(km_at(p) == 0.0, 0.0, temp_far(p))

    return ts_at, km_at, km_halo, temp_far, ahead


def still_plane(ts_at, km_at, p, fx_low, fx_high):
    k, t = km_at(p), ts_at(p)
    ext, ny = k.shape
    k_low, k_high = pltpu.roll(k, 1, 1), pltpu.roll(k, ny - 1, 1)
    count = jnp.where(k_low == 0.0, 1.0, 0.0) + jnp.where(k_high == 0.0, 1.0, 0.0)
    y_low, y_high = face(k, k_low), face(k, k_high)
    k_low, k_high = pltpu.roll(k, 1, 0), pltpu.roll(k, ext - 1, 0)
    count = count + (jnp.where(k_low == 0.0, 1.0, 0.0) + jnp.where(k_high == 0.0, 1.0, 0.0))
    z_low = face(k, k_low)
    z_high = pltpu.roll(z_low, ext - 1, 0)
    total = (y_low + y_high) + (z_low + z_high)
    near = spread_in_plane(t, y_low, y_high, z_low, z_high)
    for fx, q in ((fx_low, p - 1), (fx_high, p + 1)):
        if fx is not None:
            count = count + jnp.where(km_at(q) == 0.0, 1.0, 0.0)
            total = total + fx
            near = near + fx * ts_at(q)
    return y_low, y_high, z_low, z_high, 1.0 + total, near - (FILM * count + total) * t


def spread_in_plane(v, y_low, y_high, z_low, z_high):
    ext, ny = v.shape
    in_y = y_low * pltpu.roll(v, 1, 1) + y_high * pltpu.roll(v, ny - 1, 1)
    in_z = z_low * pltpu.roll(v, 1, 0) + z_high * pltpu.roll(v, ext - 1, 0)
    return in_z + in_y


def spread(v, below, above, fx_low, fx_high, *faces):
    return (fx_low * below + fx_high * above) + spread_in_plane(v, *faces)


def static_body(tsm, km, theirs, fx, *outs):
    nx = tsm.shape[0]
    ts_at, km_at = reader(nx, None, None, tsm, km, theirs)[:2]
    first = DEEP + 1
    for n in range(nx - 1):
        fx[n] = face(km_at(first + n), km_at(first + n - 1))
    for n in range(nx - 2):
        for out, v in zip(outs, still_plane(ts_at, km_at, first + n, fx[n], fx[n + 1])):
            out[n] = v


def conduct_body(*all_refs):
    early_cross, early_intra, late_cross, late_intra, theirs, joined, bounce = all_refs[0:7]
    in_fx, in_still = all_refs[7], all_refs[8:14]
    tsm, km, hot, ts, corners, heat_in, pops_in, new_heat, new_pops, new_solid = all_refs[14:24]
    temp, resid, step_a, step_b, fx = all_refs[24:29]
    still, (total, ends, patched, sems) = all_refs[29:35], all_refs[35:]
    nx, nz, ny = ts.shape
    planes, ext = temp.shape[:2]
    tiles = nz // TILE
    own = slice(0, nz)
    early, late = picker(early_cross, early_intra), picker(late_cross, late_intra)
    ts_at, km_at, km_halo, temp_far, ahead = reader(nx, early, late, tsm, km, theirs)

    def ready(p):
        return DEEP < p < DEEP + nx - 1

    def fx_at(p):
        if p in (1, planes - 1):
            return None
        return in_fx[p - DEEP - 1] if DEEP < p < DEEP + nx else fx[p]

    def still_at(n, p):
        return in_still[n][p - DEEP - 1] if ready(p) else still[n][p]

    def apply(v, p, now):
        near = spread(v, now[p - 1], now[p + 1], fx_at(p), fx_at(p + 1), *(still_at(n, p) for n in range(4)))
        return near - still_at(4, p) * v

    def temp_at(p):
        return joined[p - DEEP] if DEEP <= p < DEEP + nx else temp_far(p)

    def sent(n, side):
        return jnp.concatenate([early(side, ahead + n * tiles, tiles), late(side, 3 * HALO + 2 + n, 1)], axis=0)

    def mine(n, side):
        end = (hot[2 - side, side * (nx - 1)], bounce[side])[n]
        return jnp.concatenate([end, theirs[2 * nx + 2 * n + side]], axis=0)

    def join(side):
        p_own = DEEP + side * (nx - 1)
        p_far = p_own - 1 + 2 * side
        t_own, t_far = ts_at(p_own), ts_at(p_far)
        got = jnp.where(t_far == 0.0, sent(0, side), mine(1, side) + WALL_NEAR * t_far)
        back = jnp.where(t_own == 0.0, mine(0, side), sent(1, side) + WALL_NEAR * t_own)
        temp[p_own] = jnp.where(t_own == 0.0, temp_at(p_own) + got, 0.0)
        temp[p_far] = jnp.where(t_far == 0.0, temp_at(p_far) + back, 0.0)
        return got

    row = rows8((TILE, ny))
    corner = 3 * HALO + 4
    copies = []
    for n, (d, x, p, side) in enumerate(
        (
            (11, 0, DEEP - 1, 0),
            (13, 0, DEEP - 1, 0),
            (12, nx - 1, DEEP + nx, 1),
            (14, nx - 1, DEEP + nx, 1),
        )
    ):
        by, at, rows = (1, 0, slice(0, TILE)) if DIRS[d][2] > 0 else (TILE - 1, TILE - 1, slice(nz - TILE, nz))
        there = pltpu.roll(km_halo(p), by, 0)
        both = (row == at) & (tsm[x, rows, :] == 0.0) & (there == 0.0)
        patched[n] = jnp.where(both, pltpu.roll(late(side, corner, 1), by, 0), corners[n])
        copies.append(pltpu.make_async_copy(patched.at[n], new_pops.at[d, x, rows, :], sems.at[n]))
        copies[-1].start()
    for p in range(1, planes - 1):
        if p not in (DEEP - 1, DEEP, DEEP + nx - 1, DEEP + nx):
            temp[p] = jnp.where(km_at(p) == 0.0, temp_at(p), 0.0)
    up, down = join(0), join(1)
    ends[0] = jnp.where(tsm[0] == 0.0, up[own], hot[1, 0])
    ends[1] = jnp.where(tsm[nx - 1] == 0.0, down[own], hot[2, nx - 1])
    for n, (d, x) in enumerate(((1, 0), (2, nx - 1))):
        copies.append(pltpu.make_async_copy(ends.at[n], new_heat.at[d, x], sems.at[4 + n]))
        copies[-1].start()

    for p in range(2, planes - 1):
        if not DEEP < p < DEEP + nx:
            fx[p] = face(km_at(p), km_at(p - 1))
    for p in range(1, planes - 1):
        if not ready(p):
            for out, v in zip(still, still_plane(ts_at, km_at, p, fx_at(p), fx_at(p + 1))):
                out[p] = v

    def residual(p):
        mid = temp[p]
        near = pltpu.roll(mid, 1, 0) + pltpu.roll(mid, ext - 1, 0)
        for q in (p - 1, p + 1):
            if 0 < q < planes - 1:
                near = near + temp[q]
        near = near + (pltpu.roll(mid, 1, 1) + pltpu.roll(mid, ny - 1, 1))
        r = jnp.where(km_at(p) == 0.0, 0.0, FILM * near) + still_at(5, p)
        if p in (1, planes - 2):
            side = int(p > 1)
            middle = early(side, ahead + (2 * tiles) + HALO * (tiles - 2), tiles - 2)
            ends_of = late(side, 3 * HALO, 2)
            open_rows = jnp.zeros((TILE, ny), jnp.float32)
            r = r + jnp.concatenate([ends_of[0:TILE], middle, ends_of[TILE:], open_rows], axis=0)
        return r

    def pairs(start):
        every = list(range(start, planes - start))
        return [every[n : n + 2] for n in range(0, len(every), 2)]

    for group in pairs(1):
        for p, r in [(p, residual(p)) for p in group]:
            resid[p] = r
            s = r * (1.0 / THETA)
            step_a[p] = s
            if DEEP <= p < DEEP + nx:
                total[p - DEEP] = ts[p - DEEP] + s[own]
    sigma = THETA / DELTA
    ratio = 1.0 / sigma
    now, later = step_a, step_b
    for sweep in range(1, ITERS):
        after = 1.0 / (2.0 * sigma - ratio)
        for group in pairs(1 + sweep):
            done = []
            for p in group:
                v = now[p]
                r = resid[p] + apply(v, p, now)
                done.append((p, r, (after * ratio) * v + (2.0 * after / DELTA) * r))
            for p, r, s in done:
                if sweep + 1 < ITERS:
                    resid[p] = r
                    later[p] = s
                if DEEP <= p < DEEP + nx:
                    x = p - DEEP
                    total[x] = total[x] + s[own]
                    if sweep + 1 == ITERS:
                        copies.append(pltpu.make_async_copy(total.at[x], new_solid.at[x], sems.at[6 + x]))
                        copies[-1].start()
        ratio = after
        now, later = later, now
    for copy in copies:
        copy.wait()


FLOW_DIRS = (
    (0, 1, 2, 3, 4, 7, 8, 9, 10),
    (5, 6, 11, 12, 13, 14, 15, 16, 17, 18),
    tuple(range(19)),
)
FLOW_RUNS = (((0, 5), (7, 4)), ((5, 2), (11, 8)), ((0, 19),))


def flow_body(part, *all_refs):
    early = theirs = None
    if part == 0:
        flow, tsm, out, turned, buf, sems = all_refs
    elif part == 1:
        flow, tsm, theirs, flow_rows, turned, heat, heat_ends, held, out, heat_out, buf, sems, heat_sems = all_refs
    else:
        flow, tsm, theirs, flow_rows, turned, early_cross, early_intra, held, out, corners, buf, sems = all_refs
        early = picker(early_cross, early_intra)
    nx, nz, ny = flow.shape[1:]
    tiles = nz // TILE
    row = rows8((TILE, ny))
    if part == 0:
        for x in range(nx):
            for n, by in enumerate((1, ny - 1)):
                turned[n, x] = pltpu.roll(tsm[x], by, 1)
    if part == 1:
        copy_heat = pltpu.make_async_copy(heat, heat_out, heat_sems.at[0])
        copy_heat.start()

    def span(i):
        return slice(i * TILE, (i + 1) * TILE)

    def turn(v, cy):
        return pltpu.roll(v, cy % ny, 1) if cy else v

    def shift(tile, i, cz):
        if not cz:
            return tile(i)
        far, by = (0, 1) if cz > 0 else (TILE - 1, TILE - 1)
        return jnp.where(row == far, pltpu.roll(tile(i - cz), by, 0), pltpu.roll(tile(i), by, 0))

    def mask_tile(q, cy, i):
        if not 0 <= q < nx:
            return turn(early(int(q > 0), (0 if q > 0 else HALO - 1) * tiles + i % tiles, 1), cy)
        if not 0 <= i < tiles:
            return turn(theirs[2 * nx + 4 + q], cy)
        if cy:
            return turned[0 if cy > 0 else 1, q, span(i), :]
        return tsm[q, span(i), :]

    def flow_tile(d, q, i):
        if 0 <= q < nx:
            if 0 <= i < tiles:
                return flow[d, q, span(i), :]
            v = theirs[nx + q] if d in (11, 12, 13, 14) else flow_rows[q]
            by = ZSLOT[d] if DIRS[d][2] > 0 else TILE - ZSLOT[d]
            return pltpu.roll(v, by % TILE, 0) if by % TILE else v
        side, n = (0, XHIGH.index(d)) if q < 0 else (1, XLOW.index(d))
        return early(side, (HALO + n) * tiles + i % tiles, 1)

    copies = []
    for at, x in enumerate(range(1, nx - 1) if part < 2 else (0, nx - 1)):
        slot = at
        for i in range(tiles):
            is_pore = tsm[x, span(i), :] == 0.0
            done = []
            for at_d, d in enumerate(FLOW_DIRS[part]):
                if d == 0:
                    done.append(flow[0, x, span(i), :])
                    continue
                cx, cy, cz = DIRS[d]
                q = x - cx
                t = shift(lambda n: mask_tile(q, cy, n), i, cz)
                both = is_pore & (t == 0.0)
                v = turn(shift(lambda n: flow_tile(d, q, n), i, cz), cy)
                open_row = cz and not 0 <= q < nx and i == (0 if cz > 0 else tiles - 1)
                if open_row:
                    both = both & (row != (0 if cz > 0 else TILE - 1))
                v = jnp.where(both, v, jnp.where(is_pore, flow[OPP[d], x, span(i), :], flow[d, x, span(i), :]))
                done.append(v)
                if open_row:
                    corners[(11, 13, 12, 14).index(d)] = v
            for at_d, v in enumerate(done):
                buf[slot, at_d, span(i), :] = v
        begin = 0
        copies.append([])
        for n, (d, count) in enumerate(FLOW_RUNS[part]):
            src, dst = buf.at[slot, begin : begin + count], out.at[d : d + count, x]
            copies[-1].append(pltpu.make_async_copy(src, dst, sems.at[2 * slot + n]))
            copies[-1][-1].start()
            begin += count
    if part == 1:
        copy_heat.wait()
        for n, rows in ((0, slice(0, TILE)), (1, slice(nz - TILE, nz))):
            copy = pltpu.make_async_copy(heat_ends.at[n], heat_out.at[5 + n, :, rows, :], heat_sems.at[n])
            copy.start()
            copies[-1].append(copy)
    for group in copies:
        for copy in group:
            copy.wait()


def ring(axis, by):
    count = lax.axis_size(axis)
    return [(i, (i + by) % count) for i in range(count)]


def along_z(rows):
    if lax.axis_size("grp") == 2:
        return lax.ppermute(rows, "grp", ring("grp", 1))
    from_below = lax.ppermute(rows, "grp", ring("grp", 1))
    from_above = lax.ppermute(rows, "grp", ring("grp", -1))
    upper = lax.broadcasted_iota(jnp.int32, rows.shape, 1) < DEEP
    return jnp.where(upper, from_above, from_below)


def along_x(cross, intra):
    count = lax.axis_size("dev")
    across = [(i, (i + 2 * (i % 2) - 1) % count) for i in range(count)]
    return lax.ppermute(cross, "dev", across), lax.ppermute(intra, "dev", [(i, i ^ 1) for i in range(count)])


def per_device(populations, heat_pops, solid_temp, conductivity, pore_mask):
    nx, nz, ny = solid_temp.shape
    ext = nz + TILE
    tiles = ext // TILE
    planes = nx + 2 * DEEP
    field = (nx, nz, ny)
    wide = (planes, ext, ny)
    dma = pltpu.SemaphoreType.DMA
    flow, hot, tsm, km, my_rows = call(
        collide_body,
        [(19, *field), (7, *field), field, field, (nx, TILE, ny)],
        [pltpu.with_memory_space_constraint(v, pltpu.HBM) for v in (populations, heat_pops, solid_temp, conductivity, pore_mask)],
        in_specs=[HBM] * 5,
        scratch=[
            pltpu.VMEM((19, *field), jnp.float32),
            pltpu.VMEM((7, *field), jnp.float32),
            pltpu.VMEM(field, jnp.float32),
            pltpu.VMEM(field, jnp.float32),
            pltpu.VMEM(field, jnp.int32),
            dma((3 + 2 * nx,)),
        ],
        limit=12 << 20,
        us=4,
    )
    new_heat, temp, bounce, zmsg, zflow = call(
        heat_body,
        [(7, *field), field, (2, nz, ny), (3 * nx + 4, TILE, ny), (nx, TILE, ny)],
        [hot, flow, tsm, my_rows],
    )
    theirs = along_z(zmsg)
    flow_rows = along_z(zflow)
    early_shape = ((HALO + len(XLOW) + 2) * (tiles - 1) + DEEP * (tiles - 3), TILE, ny)
    early = along_x(*call(early_body, [early_shape] * 2, [km, flow, hot, bounce, temp]))

    def flow_call(part, outs, args, out_specs, in_hbm=0, extra=(), **rest):
        held = (2 if part == 2 else nx - 2, len(FLOW_DIRS[part]), nz, ny)
        return call(
            functools.partial(flow_body, part),
            outs,
            args,
            in_specs=[VM] * (len(args) - in_hbm) + [ANY] * in_hbm,
            out_specs=out_specs,
            scratch=[pltpu.VMEM(held, jnp.float32), dma((2 * nx,)), *extra],
            limit=6 << 20,
            **rest,
        )

    pops_shape, heat_shape = (19, *field), (7, *field)
    new_pops, turned = flow_call(0, [pops_shape, (2, *field)], [flow, tsm], [ANY, VM], us=20)
    late_shape = (4 * HALO + 5, TILE, ny)
    heat_ends, joined, cross, intra = call(
        zjoin_body,
        [(2, nx, TILE, ny), (nx, ext, ny), late_shape, late_shape],
        [zmsg, theirs, temp, km, new_heat, turned],
        us=50,
    )
    late = along_x(cross, intra)
    new_pops, new_heat = flow_call(
        1,
        [pops_shape, heat_shape],
        [flow, tsm, theirs, flow_rows, turned, new_heat, heat_ends, new_pops],
        [ANY, ANY],
        in_hbm=1,
        extra=[dma((2,))],
        aliases={7: 0},
        us=20,
    )
    new_pops, corners = flow_call(
        2,
        [pops_shape, (4, TILE, ny)],
        [flow, tsm, theirs, flow_rows, turned, *early, new_pops],
        [ANY, VM],
        in_hbm=1,
        aliases={7: 0},
    )
    fixed = call(
        static_body,
        [(nx - 1, ext, ny)] + [(nx - 2, ext, ny)] * 6,
        [tsm, km, theirs],
    )
    new_heat, new_pops, new_solid = call(
        conduct_body,
        [heat_shape, pops_shape, field],
        [*early, *late, theirs, joined, bounce, *fixed, tsm, km, hot, solid_temp, corners, new_heat, new_pops],
        in_specs=[VM] * 19 + [ANY] * 2,
        out_specs=[ANY, ANY, ANY],
        scratch=[pltpu.VMEM(wide, jnp.float32)] * 11
        + [pltpu.VMEM(field, jnp.float32), pltpu.VMEM((2, nz, ny), jnp.float32), pltpu.VMEM((4, TILE, ny), jnp.float32)]
        + [dma((6 + nx,))],
        aliases={19: 0, 20: 1},
        limit=12 << 20,
        us=4,
    )
    return new_pops, new_heat, new_solid


def solution(mesh):
    wide = P(None, "dev", "grp", None)
    flat = P("dev", "grp", None)
    return jax.shard_map(
        per_device,
        mesh=mesh,
        in_specs=(wide, wide, flat, flat, flat),
        out_specs=(wide, wide, flat),
        check_vma=False,
    )
```
